32 devices in a mesh: tiles: 8 (over y, x, core), slab: 4 (over z).
Axes of the slice: x: 2, y: 2, z: 4, core: 2. Of those that a mesh axis runs over, the one named last changes fastest.
Arguments:
- adjoint: float32 [4, 3, 32, 8100], P('slab', None, 'tiles'), may hold values from -6 to 6
- state: float32 [4, 3, 32, 8100], P('slab', None, 'tiles'), may hold values from 0.1 to 10
- weights: float32 [4, 32, 8100], P('slab', 'tiles'), may hold values from 0.02 to 0.24
- vertical: float32 [4, 32, 8100], P('slab', 'tiles'), may hold values from 0.02 to 0.3
- mask: int32 [4, 32, 8100], P('slab', 'tiles'), may hold values 0 or 1
- rate: float32 [3, 32, 8100], P(None, 'tiles'), may hold values from 0.005 to 0.1
- neighbours: int32 [32, 4], P('tiles'), may hold values from -1 to 31, as said below
- links: int32 [32, 4], P('tiles'), may hold values from 0 to 7, as said below
- owners: int32 [32], replicated, may hold values from 0 to 7
Outputs:
- adjoint_out: float32 [4, 3, 32, 8100], P('slab', None, 'tiles')
- control_gradient: float32 [4, 8, 675], P('slab', 'tiles')
The draws below stay inside these ranges and needn't reach their ends.
Inputs may be any that keep to these rules, and one draw needn't show every extreme that they name: Tiles are placed row by row in a layout of 8 columns, tile t at position t + 2: neighbours[t, s] is t - 8, t + 8, t - 1, t + 1 or -1, and links are mutual: if neighbours[t, s] = u >= 0 then neighbours[u, links[t, s] // 2] = t and links[u, links[t, s] // 2] = 2 s + links[t, s] % 2. `links`: 0 where the side is closed; odd only across the seam between the faces and the cap.
All inputs are finite; a program needn't handle non-finite values. No bound on the sum of `mask` on one device may be relied on, other than what follows from the above.
Results may differ from the reference program's by a relative error of at most 0.000071.
Values sent between devices are 32-bit elements; how exact they have to be, the bound alone decides.
No kernel may reach another device: no remote copies, remote signals or barrier semaphores. Data moves between devices by JAX's collectives and lax.ppermute only.
A program may use at most 64 MiB of HBM per device.

```python
import math
import jax
import jax.numpy as jnp
from jax import lax

TILE = 90
TRACERS = 3
LEVELS = 4
SUBSTEPS = 2
BLOCK = 6
ROW_TILES = 8
TILES_DEV = 4
TILES_ALL = 32
COARSE = 15
OWNERS = 8


def tile_layout(key):
    rows = (TILES_ALL + 2 + ROW_TILES - 1) // ROW_TILES
    first, second, third = jax.random.split(jax.random.fold_in(key, 11), 3)
    shut_across = jax.random.randint(first, (rows, ROW_TILES - 1), 0, 2) == 0
    shut_along = jax.random.randint(second, (max(rows - 1, 1), ROW_TILES), 0, 2) == 0
    seam = jax.random.randint(third, (), 3, 7).astype(jnp.int32)
    index = jnp.arange(TILES_ALL, dtype=jnp.int32)
    position = index + 2
    row_of = position // ROW_TILES
    col_of = position % ROW_TILES
    turned = col_of >= seam
    drawn_dr = jnp.array([-1, 1, 0, 0], jnp.int32)
    drawn_dc = jnp.array([0, 0, -1, 1], jnp.int32)
    turned_dr = jnp.array([0, 0, 1, -1], jnp.int32)
    turned_dc = jnp.array([-1, 1, 0, 0], jnp.int32)
    step_r = jnp.where(turned[:, None], turned_dr[None, :], drawn_dr[None, :])
    step_c = jnp.where(turned[:, None], turned_dc[None, :], drawn_dc[None, :])
    near_r = row_of[:, None] + step_r
    near_c = col_of[:, None] + step_c
    near_pos = near_r * ROW_TILES + near_c
    inside = (near_r >= 0) & (near_r < rows) & (near_c >= 0) & (near_c < ROW_TILES)
    inside = inside & (near_pos >= 2) & (near_pos < TILES_ALL + 2)
    edge_c = jnp.clip(jnp.minimum(col_of[:, None], near_c), 0, ROW_TILES - 2)
    edge_r = jnp.clip(jnp.minimum(row_of[:, None], near_r), 0, max(rows - 2, 0))
    row_here = jnp.broadcast_to(row_of[:, None], edge_c.shape)
    col_here = jnp.broadcast_to(col_of[:, None], edge_c.shape)
    closed = jnp.where(step_r == 0, shut_across[row_here, edge_c], shut_along[edge_r, col_here])
    target = near_pos - 2
    middle = TILES_ALL // 2
    own_middle = (index >= middle) & (index < middle + TILES_DEV)
    touches = own_middle[:, None] | (target >= middle) & (target < middle + TILES_DEV)
    middle_row = (middle + 2) // ROW_TILES
    seam_edge = (step_r == 0) & (row_here == middle_row) & (edge_c == seam - 1)
    opened = inside & (jnp.logical_not(closed) | touches | seam_edge)
    back_r = -step_r
    back_c = -step_c
    near_turned = near_c >= seam
    drawn_side = jnp.where(back_r == -1, 0, jnp.where(back_r == 1, 1, jnp.where(back_c == -1, 2, 3)))
    turned_side = jnp.where(back_c == -1, 0, jnp.where(back_c == 1, 1, jnp.where(back_r == 1, 2, 3)))
    back_side = jnp.where(near_turned, turned_side, drawn_side)
    flipped = (near_turned != turned[:, None]).astype(jnp.int32)
    neighbours = jnp.where(opened, target, -1).astype(jnp.int32)
    links = jnp.where(opened, back_side * 2 + flipped, 0).astype(jnp.int32)
    return (neighbours, links)


def draw_neighbours(key, part):
    return tile_layout(key)[0]


def draw_links(key, part):
    return tile_layout(key)[1]


def touch_ends(result, rng, low, top_value):
    longest = result.shape.index(max(result.shape))
    spots = []
    for shift in (0, 1):
        where = [jax.random.randint(jax.random.fold_in(rng, axis), (), 0, length) for axis, length in enumerate(result.shape)]
        where[longest] = (where[longest] + shift) % result.shape[longest]
        spots.append(tuple(where))
    return result.at[spots[0]].set(low).at[spots[1]].set(top_value)


def block_scale(rng, dims, shards, smallest, largest):
    loudness = 1.0
    for dim, shards_of in shards:
        steps = jax.random.uniform(jax.random.fold_in(jax.random.fold_in(rng, 6), dim), (shards_of,), jnp.float32, smallest / len(shards), largest / len(shards))
        loudness = loudness * jnp.repeat(jnp.exp(steps), dims[dim] // shards_of).reshape((-1,) + (1,) * (len(dims) - 1 - dim))
    return loudness


def bell_draw(stream_key, dims, deviation, most, cuts=(), kind=jnp.bfloat16):
    drawn = deviation * jax.random.normal(stream_key, dims, jnp.float32)
    if cuts:
        drawn = drawn * block_scale(stream_key, dims, cuts, -0.22, 0.18)
    return jnp.clip(drawn, -most, most).astype(kind)


def setup_inputs(seed: int = 0) -> dict:
    streams_of = jax.random.split(jax.random.key(seed), 10)
    return {
        "adjoint": bell_draw(streams_of[0], (LEVELS, TRACERS, TILES_ALL, TILE * TILE), 1.0, 6.0, ((0, 4), (2, 8)), jnp.float32),
        "state": jnp.clip(jnp.exp(math.log(10.0) - 4.6051702 * jax.random.uniform(streams_of[1], (LEVELS, TRACERS, TILES_ALL, TILE * TILE), jnp.float32) ** block_scale(streams_of[1], (LEVELS, TRACERS, TILES_ALL, TILE * TILE), ((0, 4), (2, 8)), -0.2, 0.2)), 0.1, 10.0),
        "weights": jnp.clip(jnp.exp(math.log(0.24) - 2.4849066 * jax.random.uniform(streams_of[2], (LEVELS, TILES_ALL, TILE * TILE), jnp.float32) ** block_scale(streams_of[2], (LEVELS, TILES_ALL, TILE * TILE), ((0, 4), (1, 8)), -0.2, 0.2)), 0.02, 0.24),
        "vertical": jnp.clip(jnp.exp(math.log(0.3) - 2.7080503 * jax.random.uniform(streams_of[3], (LEVELS, TILES_ALL, TILE * TILE), jnp.float32) ** block_scale(streams_of[3], (LEVELS, TILES_ALL, TILE * TILE), ((0, 4), (1, 8)), -0.2, 0.2)), 0.02, 0.3),
        "mask": touch_ends((jax.random.randint(streams_of[4], (LEVELS, TILES_ALL, TILE * TILE), 0, 4) < 3).astype(jnp.int32), jax.random.fold_in(streams_of[4], 1), 0, 1),
        "rate": jnp.clip(jnp.exp(math.log(0.1) - 2.9957323 * jax.random.uniform(streams_of[5], (TRACERS, TILES_ALL, TILE * TILE), jnp.float32) ** block_scale(streams_of[5], (TRACERS, TILES_ALL, TILE * TILE), ((1, 8),), -0.2, 0.2)), 0.005, 0.1),
        "neighbours": draw_neighbours(jax.random.fold_in(streams_of[9], 71), 0),
        "links": draw_links(jax.random.fold_in(streams_of[9], 71), 0),
        "owners": touch_ends(jax.random.randint(streams_of[8], (TILES_ALL,), 0, OWNERS), jax.random.fold_in(streams_of[8], 1), 0, OWNERS - 1).astype(jnp.int32),
    }


def edge_rows(field):
    return jnp.concatenate((field[..., 0, :], field[..., -1, :], field[..., :, 0], field[..., :, -1]), axis=-1)


def pick_halo(edge_all, neighbours, links):
    width = edge_all.shape[-1] // 4
    grid = edge_all.reshape(edge_all.shape[:-1] + (4, width))
    source = jnp.maximum(neighbours, 0)
    picked = grid[..., source, links // 2, :]
    picked = jnp.where((links % 2)[..., None] == 1, picked[..., ::-1], picked)
    return jnp.where(neighbours[..., None] >= 0, picked, jnp.float32(0.0))


def neighbour_sum(field, halo):
    upper = jnp.concatenate((halo[..., 0, :][..., None, :], field[..., :-1, :]), axis=-2)
    lower = jnp.concatenate((field[..., 1:, :], halo[..., 1, :][..., None, :]), axis=-2)
    left_side = jnp.concatenate((halo[..., 2, :][..., :, None], field[..., :, :-1]), axis=-1)
    right_side = jnp.concatenate((field[..., :, 1:], halo[..., 3, :][..., :, None]), axis=-1)
    return upper + lower + left_side + right_side


def reference(adjoint, state, weights, vertical, mask, rate, neighbours, links, owners):
    count_all = adjoint.shape[2]
    shape_four = (LEVELS, count_all, TILE, TILE)
    lam = adjoint.reshape(LEVELS, TRACERS, count_all, TILE, TILE)
    wet = mask.astype(jnp.float32).reshape(shape_four)
    mixing = wet * weights.reshape(shape_four)
    count = neighbour_sum(wet, pick_halo(edge_rows(wet), neighbours, links))
    zero_level = jnp.zeros((1, count_all, TILE, TILE), jnp.float32)
    wet_above = jnp.concatenate((zero_level, wet[:-1]), axis=0)
    above = vertical.reshape(shape_four) * wet * wet_above
    below = jnp.concatenate((above[1:], zero_level), axis=0)
    uptake = 1.0 - rate.reshape(1, TRACERS, count_all, TILE, TILE)
    zero_tracers = jnp.zeros((1, TRACERS, count_all, TILE, TILE), jnp.float32)
    for step in range(SUBSTEPS):
        spread = mixing[:, None] * lam
        halo = pick_halo(edge_rows(spread), neighbours, links)
        horizontal = lam * (1.0 - (mixing * count)[:, None]) + wet[:, None] * neighbour_sum(spread, halo)
        taken = horizontal * uptake
        from_above = jnp.concatenate((zero_tracers, taken[:-1]), axis=0)
        from_below = jnp.concatenate((taken[1:], zero_tracers), axis=0)
        lam = taken + above[:, None] * (from_above - taken) + below[:, None] * (from_below - taken)
    term = wet[:, None] * lam * state.reshape(LEVELS, TRACERS, count_all, TILE, TILE)
    term = term.reshape(LEVELS, TRACERS, count_all, COARSE, BLOCK, COARSE, BLOCK).sum(axis=(4, 6))
    onehot = (owners[:, None] == jnp.arange(OWNERS, dtype=jnp.int32)[None, :]).astype(jnp.float32)
    gradient = jnp.einsum("lctyx,tk->lkcyx", term, onehot, precision=lax.Precision.HIGHEST)
    return lam.reshape(LEVELS, TRACERS, count_all, TILE * TILE), gradient.reshape(LEVELS, OWNERS, TRACERS * COARSE * COARSE)
```

```python
import functools

import jax
import jax.numpy as jnp
from jax import lax
from jax.experimental import pallas as pl
from jax.experimental.pallas import tpu as pltpu
from jax.sharding import PartitionSpec as P

TILE = 90
CELLS = TILE * TILE
SUBSTEPS = 2
BLOCK = 6
COARSE = 15
LANES = 128
COLS = 32
HALF = COLS * LANES
TILES = 4
SIDES = 4
SPOTS = TILES * SIDES
F32 = jnp.float32
I32 = jnp.int32


def position():
    lane = lax.broadcasted_iota(I32, (8, LANES), 1)
    low = lax.broadcasted_iota(I32, (8, LANES), 0) < TILES
    return lane, low


def cell_at(lane, low, v):
    cell = lane + jnp.where(low, 0, HALF) + v * LANES
    y = (cell * 46604) >> 22
    return cell - y * TILE, y


def lane_gather(values, index):
    return jnp.take_along_axis(values, index, axis=1, mode="promise_in_bounds")


def fold(read, write):
    for v in range(COLS):
        write(v, 0, read(v * LANES, LANES))
        start = HALF + v * LANES
        width = min(LANES, CELLS - start)
        part = read(start, width)
        if width < LANES:
            part = jnp.concatenate([part, jnp.zeros((TILES, LANES - width), F32)], axis=1)
        write(v, TILES, part)


def set_guards(ref, plane, low):
    first, last = ref[plane, 1], ref[plane, COLS]
    ref[plane, 0] = jnp.where(low, 0.0, pltpu.roll(last, TILES, 0))
    ref[plane, COLS + 1] = jnp.where(low, pltpu.roll(first, TILES, 0), 0.0)


def inner_sum(ref, plane, v, lane, west, east):
    before, here, after = ref[plane, v], ref[plane, v + 1], ref[plane, v + 2]
    left = pltpu.roll(jnp.where(lane < LANES - 1, here, before), 1, 1)
    right = pltpu.roll(jnp.where(lane >= 1, here, after), LANES - 1, 1)
    up = pltpu.roll(jnp.where(lane < LANES - TILE, here, before), TILE, 1)
    down = pltpu.roll(jnp.where(lane >= TILE, here, after), LANES - TILE, 1)
    return jnp.where(west, 0.0, left) + jnp.where(east, 0.0, right) + (up + down)


def edge_sides(load, planes, lane, low):
    base = TILE * lane - jnp.where(low, 0, HALF)
    index = [(base + shift) & (LANES - 1) for shift in (0, TILE - 1)]
    column = [(base + shift) >> 7 for shift in (0, TILE - 1)]

    def body(v, found):
        hit = [c == v for c in column]
        out = []
        for p in range(planes):
            values = load(p, v)
            for k in range(2):
                out.append(jnp.where(hit[k], lane_gather(values, index[k]), found[2 * p + k]))
        return tuple(out)

    found = lax.fori_loop(0, COLS, body, tuple(jnp.zeros((8, LANES), F32) for _ in range(2 * planes)), unroll=4)
    bottom = CELLS - TILE - HALF + lane
    out = []
    for p in range(planes):
        sides = [jnp.where(lane < TILE, load(p, 0), 0.0)[:TILES]]
        picked = jnp.where(
            (bottom >> 7) == COLS - 2,
            lane_gather(load(p, COLS - 2), bottom & (LANES - 1)),
            lane_gather(load(p, COLS - 1), bottom & (LANES - 1)),
        )
        sides.append(jnp.where(lane < TILE, picked, 0.0)[TILES:])
        for k in range(2):
            sides.append(found[2 * p + k][:TILES] + found[2 * p + k][TILES:])
        out.append(sides)
    return out


def put_sides(ref, start, sides):
    for s in range(SIDES):
        ref[pl.ds(start + s, TILES, stride=SIDES), :] = sides[s]


def halos(near_ref, link_ref, all_ref, rows, channels, out_ref):
    sub = lax.broadcasted_iota(I32, (SPOTS, LANES), 0)
    lane = lax.broadcasted_iota(I32, (SPOTS, LANES), 1)
    turned = jnp.zeros((SPOTS, LANES), I32)
    open_ = jnp.zeros((SPOTS, LANES), I32)
    for t in range(TILES):
        for s in range(SIDES):
            spot = t * SIDES + s
            near, link = near_ref[t, s], link_ref[t, s]
            tile = jnp.maximum(near, 0)
            row = (tile // TILES) * (3 * rows) + (tile % TILES) * SIDES + link // 2
            for level in range(3):
                out_ref[pl.ds(level * rows + spot, channels, stride=SPOTS), :] = all_ref[
                    pl.ds(row + level * rows, channels, stride=SPOTS), :
                ]
            turned = jnp.where(sub == spot, link % 2, turned)
            open_ = jnp.where(sub == spot, (near >= 0).astype(I32), open_)
    back = jnp.clip(TILE - 1 - lane, 0, LANES - 1)
    for k in range(3 * channels):
        for h in range(0, SPOTS, 8):
            at = pl.ds(k * SPOTS + h, 8)
            values = out_ref[at, :]
            values = jnp.where(turned[h : h + 8] == 1, lane_gather(values, back[h : h + 8]), values)
            keep = (open_[h : h + 8] == 1) & (lane[h : h + 8] < TILE)
            out_ref[at, :] = jnp.where(keep, values, 0.0)


def spot_rows(ref, index):
    return ref[pl.ds(index * SPOTS, SPOTS), :]


def edge_change(halo, halo_wet, edge, edge_wet, keep, mix_a, mix_b, tracers, out_ref):
    for c in range(tracers):
        parts = []
        for level in range(3):
            parts.append(keep(c) * (edge_wet(level) * halo(level, c) - edge(level, c) * halo_wet(level)))
        own, first, second = parts
        out_ref[pl.ds(c * SPOTS, SPOTS), :] = own + mix_a * (first - own) + mix_b * (second - own)


def change_planes(ref, tracers):
    out = []
    for c in range(tracers):
        sides = [ref[pl.ds(c * SPOTS + s, TILES, stride=SIDES), :] for s in range(SIDES)]
        out.append([jnp.concatenate([side, side], axis=0) for side in sides])
    return out


def add_columns(planes, v, lane, low):
    x, y = cell_at(lane, low, v)
    y = jnp.minimum(y, LANES - 1)
    west, east = x == 0, x == TILE - 1
    out = []
    for sides in planes:
        out.append(jnp.where(west, lane_gather(sides[2], y), 0.0) + jnp.where(east, lane_gather(sides[3], y), 0.0))
    return out


def add_rows(ref, planes, lane, low):
    place = (CELLS - TILE - HALF) % LANES
    for c, sides in enumerate(planes):
        ref[c, 0] = ref[c, 0] + jnp.where(low, sides[0], 0.0)
        turned = pltpu.roll(sides[1], place, 1)
        ref[c, COLS - 2] = ref[c, COLS - 2] + jnp.where(low | (lane < place), 0.0, turned)
        ref[c, COLS - 1] = ref[c, COLS - 1] + jnp.where(low | (lane >= place + TILE - LANES), 0.0, turned)


def open_kernel(adjoint_ref, weights_ref, vertical_ref, mask_ref, lam_ref, wet_ref, mixing_ref, pack_a, pack_b, spread):
    tracers = lam_ref.shape[0]
    even = lax.axis_index("slab") % 2 == 0
    head = (tracers + 1) * SPOTS

    def write_to(ref, *lead):
        def write(v, row, part):
            ref[(*lead, v, pl.ds(row, TILES), slice(None))] = part

        return write

    fold(lambda a, n: mask_ref[0, :, a : a + n].astype(F32), write_to(wet_ref))
    fold(lambda a, n: weights_ref[0, :, a : a + n], write_to(mixing_ref))
    fold(lambda a, n: vertical_ref[0, :, a : a + n], write_to(spread, tracers))
    for c in range(tracers):
        fold(lambda a, n, c=c: adjoint_ref[0, c, :, a : a + n], write_to(lam_ref, c))
    lane, low = position()

    def body(v, carry):
        wet = wet_ref[v]
        mixing = wet * mixing_ref[v]
        mixing_ref[v] = mixing
        for c in range(tracers):
            spread[c, v] = mixing * lam_ref[c, v]
        vertical = spread[tracers, v]
        at = pl.ds(head + v * 8, 8)
        pack_a[at, :] = wet * jnp.where(even, 1.0, vertical)
        pack_b[at, :] = wet * jnp.where(even, vertical, 1.0)
        spread[tracers, v] = wet
        return carry

    lax.fori_loop(0, COLS, body, 0, unroll=4)
    found = edge_sides(lambda p, v: spread[p, v], tracers + 1, lane, low)
    for p in range(tracers + 1):
        put_sides(pack_a, p * SPOTS, found[p])
        put_sides(pack_b, p * SPOTS, found[p])


def inner_first_kernel(lam_ref, wet_ref, mixing_ref, rate_ref, out_ref, stay_ref, keep_ref, spread):
    tracers = lam_ref.shape[0]
    lane, low = position()
    for c in range(tracers):

        def write(v, row, part, c=c):
            keep_ref[c, v, pl.ds(row, TILES), :] = 1.0 - part

        fold(lambda a, n, c=c: rate_ref[c, :, a : a + n], write)

    def fill(v, carry):
        mixing = mixing_ref[v]
        for c in range(tracers):
            spread[c, v + 1] = mixing * lam_ref[c, v]
        spread[tracers, v + 1] = wet_ref[v]
        return carry

    lax.fori_loop(0, COLS, fill, 0, unroll=4)
    for c in range(tracers + 1):
        set_guards(spread, c, low)

    def body(v, carry):
        x, _ = cell_at(lane, low, v)
        west, east = x == 0, x == TILE - 1
        wet = wet_ref[v]
        stay = 1.0 - mixing_ref[v] * inner_sum(spread, tracers, v, lane, west, east)
        stay_ref[v] = stay
        for c in range(tracers):
            moved = inner_sum(spread, c, v, lane, west, east)
            out_ref[c, v] = (lam_ref[c, v] * stay + wet * moved) * keep_ref[c, v]
        return carry

    lax.fori_loop(0, COLS, body, 0, unroll=2)


def inner_kernel(lam_ref, wet_ref, mixing_ref, stay_ref, keep_ref, out_ref, spread):
    tracers = lam_ref.shape[0]
    lane, low = position()

    def fill(v, carry):
        mixing = mixing_ref[v]
        for c in range(tracers):
            spread[c, v + 1] = mixing * lam_ref[c, v]
        return carry

    lax.fori_loop(0, COLS, fill, 0, unroll=4)
    for c in range(tracers):
        set_guards(spread, c, low)

    def body(v, carry):
        x, _ = cell_at(lane, low, v)
        west, east = x == 0, x == TILE - 1
        wet, stay = wet_ref[v], stay_ref[v]
        for c in range(tracers):
            moved = inner_sum(spread, c, v, lane, west, east)
            out_ref[c, v] = (lam_ref[c, v] * stay + wet * moved) * keep_ref[c, v]
        return carry

    lax.fori_loop(0, COLS, body, 0, unroll=2)


def middle_kernel(
    near_ref, link_ref, all_ref, pack_a, pack_b, got_a, got_b, taken_ref, from_a, from_b, keep_ref, mixing_ref,
    lam_ref, mix_a_ref, mix_b_ref, edge_ref, still_ref, halo_ref, change_ref, spread,
):
    tracers = lam_ref.shape[0]
    channels = tracers + 1
    rows = channels * SPOTS
    lane, low = position()
    halos(near_ref, link_ref, all_ref, rows, channels, halo_ref)

    def mix(v, carry):
        at = pl.ds(rows + v * 8, 8)
        mix_a_ref[v] = pack_a[at, :] * got_a[at, :]
        mix_b_ref[v] = pack_b[at, :] * got_b[at, :]
        return carry

    lax.fori_loop(0, COLS, mix, 0, unroll=4)

    def load(p, v):
        if p < tracers:
            return keep_ref[p, v]
        return (mix_a_ref if p == tracers else mix_b_ref)[v]

    for p, sides in enumerate(edge_sides(load, tracers + 2, lane, low)):
        put_sides(still_ref, p * SPOTS, sides)
    for level in range(3):
        still_ref[pl.ds((tracers + 2 + level) * SPOTS, SPOTS), :] = spot_rows(halo_ref, level * channels + tracers)
    packs = (pack_a, got_a, got_b)
    edge_change(
        lambda level, c: spot_rows(halo_ref, level * channels + c),
        lambda level: spot_rows(halo_ref, level * channels + tracers),
        lambda level, c: spot_rows(packs[level], c),
        lambda level: spot_rows(packs[level], tracers),
        lambda c: spot_rows(still_ref, c),
        spot_rows(still_ref, tracers),
        spot_rows(still_ref, tracers + 1),
        tracers,
        change_ref,
    )
    planes = change_planes(change_ref, tracers)

    def body(v, carry):
        first, second = mix_a_ref[v], mix_b_ref[v]
        extra = add_columns(planes, v, lane, low)
        for c in range(tracers):
            taken = taken_ref[c, v]
            lam_ref[c, v] = taken + first * (from_a[c, v] - taken) + second * (from_b[c, v] - taken) + extra[c]
        return carry

    lax.fori_loop(0, COLS, body, 0, unroll=2)
    add_rows(lam_ref, planes, lane, low)

    def spreads(v, carry):
        for c in range(tracers):
            spread[c, v] = mixing_ref[v] * lam_ref[c, v]
        return carry

    lax.fori_loop(0, COLS, spreads, 0, unroll=4)
    for p, sides in enumerate(edge_sides(lambda p, v: spread[p, v], tracers, lane, low)):
        put_sides(edge_ref, p * SPOTS, sides)


def close_kernel(
    near_ref, link_ref, owner_ref, all_ref, pack_a, got_a, got_b, edge_ref, edge_a, edge_b, still_ref,
    taken_ref, from_a, from_b, mix_a_ref, mix_b_ref, wet_ref, state_ref,
    out_ref, part_ref, halo_ref, change_ref, lam_ref, term_ref, rows_ref, sums_ref,
):
    tracers = taken_ref.shape[0]
    rows = tracers * SPOTS
    lane, low = position()
    halos(near_ref, link_ref, all_ref, rows, tracers, halo_ref)
    packs = (pack_a, got_a, got_b)
    edges = (edge_ref, edge_a, edge_b)
    edge_change(
        lambda level, c: spot_rows(halo_ref, level * tracers + c),
        lambda level: spot_rows(still_ref, tracers + 2 + level),
        lambda level, c: spot_rows(edges[level], c),
        lambda level: spot_rows(packs[level], tracers),
        lambda c: spot_rows(still_ref, c),
        spot_rows(still_ref, tracers),
        spot_rows(still_ref, tracers + 1),
        tracers,
        change_ref,
    )
    planes = change_planes(change_ref, tracers)
    for c in range(tracers):

        def write(v, row, part, c=c):
            term_ref[c, v, pl.ds(row, TILES), :] = part

        fold(lambda a, n, c=c: state_ref[0, c, :, a : a + n], write)

    def body(v, carry):
        first, second = mix_a_ref[v], mix_b_ref[v]
        extra = add_columns(planes, v, lane, low)
        for c in range(tracers):
            taken = taken_ref[c, v]
            lam_ref[c, v] = taken + first * (from_a[c, v] - taken) + second * (from_b[c, v] - taken) + extra[c]
        return carry

    lax.fori_loop(0, COLS, body, 0, unroll=2)
    add_rows(lam_ref, planes, lane, low)

    def terms(v, carry):
        for c in range(tracers):
            term_ref[c, v] = wet_ref[v] * lam_ref[c, v] * term_ref[c, v]
        return carry

    lax.fori_loop(0, COLS, terms, 0, unroll=4)
    for c in range(tracers):
        for v in range(COLS):
            values = lam_ref[c, v]
            out_ref[0, c, :, v * LANES : (v + 1) * LANES] = values[:TILES]
            start = HALF + v * LANES
            width = min(LANES, CELLS - start)
            out_ref[0, c, :, start : start + width] = values[TILES:, :width]
        guard = pltpu.roll(term_ref[c, 0], TILES, 0)
        for block in range(COARSE):
            total = [None, None]
            for y in range(block * BLOCK, (block + 1) * BLOCK):
                half = y * TILE // HALF
                v, shift = divmod(y * TILE - half * HALF, LANES)
                values = term_ref[c, v]
                if shift + TILE > LANES:
                    after = term_ref[c, v + 1] if v + 1 < COLS else guard
                    values = jnp.where(lane >= shift, values, after)
                if shift:
                    values = pltpu.roll(values, LANES - shift, 1)
                total[half] = values if total[half] is None else total[half] + values
            parts = [total[h][h * TILES : (h + 1) * TILES] for h in range(2) if total[h] is not None]
            summed = parts[0] if len(parts) == 1 else parts[0] + parts[1]
            summed = jnp.where(lane[:TILES] < TILE, summed, 0.0)
            rows_ref[pl.ds((c * COARSE + block) * TILES, TILES), :] = summed
    lane_in = lax.broadcasted_iota(I32, (LANES, LANES), 0)
    lane_out = lax.broadcasted_iota(I32, (LANES, LANES), 1)
    low_edge = lane_out * BLOCK
    pick = ((lane_in >= low_edge) & (lane_in < low_edge + BLOCK) & (lane_out < COARSE)).astype(F32)
    sums_ref[...] = jnp.dot(rows_ref[...], pick, precision=lax.Precision.HIGHEST, preferred_element_type=F32)
    for spot in range(8):
        total = jnp.zeros((TILES, LANES), F32)
        for k in range(tracers * COARSE):
            start = k * COARSE - spot * LANES
            if start >= LANES or start + COARSE <= 0:
                continue
            values = sums_ref[pl.ds(k * TILES, TILES), :]
            values = pltpu.roll(values, start % LANES, 1) if start % LANES else values
            if start < 0:
                values = jnp.where(lane[:TILES] < start + COARSE, values, 0.0)
            elif start + COARSE > LANES:
                values = jnp.where(lane[:TILES] >= start, values, 0.0)
            total = total + values
        rows_ref[pl.ds(spot, TILES, stride=8), :] = total
    part_ref[...] = jnp.zeros_like(part_ref)
    me = lax.axis_index("tiles")
    for t in range(TILES):
        owner = owner_ref[me * TILES + t]
        part_ref[owner] = part_ref[owner] + rows_ref[pl.ds(t * 8, 8), :]


def swaps(count):
    return (
        [pair for i in range(0, count - 1, 2) for pair in ((i, i + 1), (i + 1, i))],
        [pair for i in range(1, count - 1, 2) for pair in ((i, i + 1), (i + 1, i))],
    )


def call(kernel, out, scratch, scalars=0, **kwargs):
    def run(*args):
        return pl.pallas_call(
            kernel,
            out_shape=[jax.ShapeDtypeStruct(shape, F32) for shape in out],
            in_specs=[pl.BlockSpec(memory_space=pltpu.SMEM)] * scalars
            + [pl.BlockSpec(memory_space=pltpu.VMEM)] * (len(args) - scalars),
            out_specs=[pl.BlockSpec(memory_space=pltpu.VMEM)] * len(out),
            scratch_shapes=[pltpu.VMEM(shape, F32) for shape in scratch],
            compiler_params=pltpu.CompilerParams(vmem_limit_bytes=48 * 1024 * 1024),
            name=kernel.__name__,
        )(*args)

    return run


def shards(adjoint, state, weights, vertical, mask, rate, neighbours, links, owners):
    tracers = adjoint.shape[1]
    number = lax.axis_size("tiles")
    even_swap, odd_swap = swaps(lax.axis_size("slab"))
    plane = (COLS, 8, LANES)
    planes = (tracers, *plane)
    channels = tracers + 1
    head = channels * SPOTS
    pack = (head + COLS * 8, LANES)

    lam, wet, mixing, pack_a, pack_b = call(
        open_kernel, [planes, plane, plane, pack, pack], [(channels, *plane)]
    )(adjoint, weights, vertical, mask)
    got_a = lax.ppermute(pack_a, "slab", even_swap)
    got_b = lax.ppermute(pack_b, "slab", odd_swap)
    guarded = (COLS + 2, 8, LANES)
    taken, stay, keep = call(inner_first_kernel, [planes, plane, planes], [(channels, *guarded)])(
        lam, wet, mixing, rate
    )
    from_a = lax.ppermute(taken, "slab", even_swap)
    from_b = lax.ppermute(taken, "slab", odd_swap)
    edges = lax.all_gather(jnp.stack([pack_a[:head], got_a[:head], got_b[:head]]), "tiles")
    edges = edges.reshape(number * 3 * head, LANES)
    rows = tracers * SPOTS
    lam, mix_a, mix_b, edge, still = call(
        middle_kernel,
        [planes, plane, plane, (rows, LANES), ((tracers + 5) * SPOTS, LANES)],
        [(3 * head, LANES), (rows, LANES), planes],
        2,
    )(neighbours, links, edges, pack_a, pack_b, got_a, got_b, taken, from_a, from_b, keep, mixing)
    edge_a = lax.ppermute(edge, "slab", even_swap)
    edge_b = lax.ppermute(edge, "slab", odd_swap)
    (taken,) = call(inner_kernel, [planes], [(tracers, *guarded)])(lam, wet, mixing, stay, keep)
    from_a = lax.ppermute(taken, "slab", even_swap)
    from_b = lax.ppermute(taken, "slab", odd_swap)
    edges = lax.all_gather(jnp.stack([edge, edge_a, edge_b]), "tiles")
    edges = edges.reshape(number * 3 * rows, LANES)
    out, part = call(
        close_kernel,
        [adjoint.shape, (number, 8, LANES)],
        [(3 * rows, LANES), (rows, LANES), planes, planes, (tracers * COARSE * TILES + 4, LANES), (tracers * COARSE * TILES + 4, LANES)],
        3,
    )(
        neighbours, links, owners, edges, pack_a, got_a, got_b, edge, edge_a, edge_b, still,
        taken, from_a, from_b, mix_a, mix_b, wet, state,
    )
    part = lax.all_to_all(part, "tiles", 0, 0, tiled=True)
    gradient = part.sum(axis=0).reshape(1, 1, 8 * LANES)[:, :, : tracers * COARSE * COARSE]
    return out, gradient


def solution(mesh):
    placed = (
        P("slab", None, "tiles", None),
        P("slab", None, "tiles", None),
        P("slab", "tiles", None),
        P("slab", "tiles", None),
        P("slab", "tiles", None),
        P(None, "tiles", None),
        P("tiles", None),
        P("tiles", None),
        P(),
    )
    return jax.shard_map(
        shards,
        mesh=mesh,
        in_specs=placed,
        out_specs=(P("slab", None, "tiles", None), P("slab", "tiles", None)),
        check_vma=False,
    )
```

```python
import functools

import jax
import jax.numpy as jnp
from jax import lax
from jax.experimental import pallas as pl
from jax.experimental.pallas import tpu as pltpu
from jax.sharding import PartitionSpec as P

TILE = 90
CELLS = TILE * TILE
SUBSTEPS = 2
BLOCK = 6
COARSE = 15
LANES = 128
COLS = 32
HALF = COLS * LANES
TILES = 4
SIDES = 4
SPOTS = TILES * SIDES
FIRST_HIGH = HALF // TILE
UNROLL = 8
F32 = jnp.float32
I32 = jnp.int32


def position():
    lane = lax.broadcasted_iota(I32, (8, LANES), 1)
    low = lax.broadcasted_iota(I32, (8, LANES), 0) < TILES
    return lane, low


def cell_at(lane, low, v):
    cell = lane + jnp.where(low, 0, HALF) + v * LANES
    y = (cell * 46604) >> 22
    return cell - y * TILE, y


def lane_gather(values, index):
    return jnp.take_along_axis(values, index, axis=1, mode="promise_in_bounds")


def loop(body, carry=0):
    return lax.fori_loop(0, COLS, body, carry, unroll=UNROLL)


def fold(read, write):
    for v in range(COLS):
        write(v, 0, read(v * LANES, LANES))
        start = HALF + v * LANES
        width = min(LANES, CELLS - start)
        part = read(start, width)
        if width < LANES:
            part = jnp.concatenate([part, jnp.zeros((TILES, LANES - width), F32)], axis=1)
        write(v, TILES, part)


def set_guards(ref, plane, low):
    first, last = ref[plane, 1], ref[plane, COLS]
    ref[plane, 0] = jnp.where(low, 0.0, pltpu.roll(last, TILES, 0))
    ref[plane, COLS + 1] = jnp.where(low, pltpu.roll(first, TILES, 0), 0.0)


def inner_sum(ref, plane, v, lane, west, east):
    before, here, after = ref[plane, v], ref[plane, v + 1], ref[plane, v + 2]
    left = pltpu.roll(jnp.where(lane < LANES - 1, here, before), 1, 1)
    right = pltpu.roll(jnp.where(lane >= 1, here, after), LANES - 1, 1)
    up = pltpu.roll(jnp.where(lane < LANES - TILE, here, before), TILE, 1)
    down = pltpu.roll(jnp.where(lane >= TILE, here, after), LANES - TILE, 1)
    return jnp.where(west, 0.0, left) + jnp.where(east, 0.0, right) + (up + down)


def edge_sides(load, planes, lane, low):
    step = lane & 63
    base = TILE * step + jnp.where(low, 0, FIRST_HIGH * TILE - HALF) + jnp.where(lane < 64, TILE - 1, TILE)
    index, column = base & (LANES - 1), base >> 7

    def body(v, found):
        hit = column == v
        return tuple(jnp.where(hit, lane_gather(load(p, v), index), found[p]) for p in range(planes))

    found = loop(body, tuple(jnp.zeros((8, LANES), F32) for _ in range(planes)))
    bottom = CELLS - TILE - HALF + lane
    edge = lane < TILE
    first_low = jnp.where(low, lane + 63, lane - FIRST_HIGH + 63) & (LANES - 1)
    last_low = jnp.where(low, lane, lane - FIRST_HIGH) & (LANES - 1)
    out = []
    for p in range(planes):
        top = load(p, 0)
        picked = jnp.where(
            (bottom >> 7) == COLS - 2,
            lane_gather(load(p, COLS - 2), bottom & (LANES - 1)),
            lane_gather(load(p, COLS - 1), bottom & (LANES - 1)),
        )
        west, east = lane_gather(found[p], first_low), lane_gather(found[p], last_low)
        west = jnp.where(low, jnp.where(lane == 0, top, west), west)
        west_low, east_low = west[:TILES], east[:TILES]
        here = lane[:TILES]
        west = jnp.where(here <= FIRST_HIGH, west_low, west[TILES:])
        east = jnp.where(here < FIRST_HIGH, east_low, east[TILES:])
        inside = here < TILE
        out.append(
            [
                jnp.where(inside, top[:TILES], 0.0),
                jnp.where(inside, picked[TILES:], 0.0),
                jnp.where(inside, west, 0.0),
                jnp.where(inside, east, 0.0),
            ]
        )
    return out


def put_sides(ref, start, sides):
    for s in range(SIDES):
        ref[pl.ds(start + s, TILES, stride=SIDES), :] = sides[s]


def halos(near_ref, link_ref, all_ref, rows, channels, out_ref):
    me = lax.axis_index("tiles")
    chip, core = me // 2, me % 2
    sub = lax.broadcasted_iota(I32, (SPOTS, LANES), 0)
    lane = lax.broadcasted_iota(I32, (SPOTS, LANES), 1)
    turned = jnp.zeros((SPOTS, LANES), I32)
    closed = jnp.zeros((SPOTS, LANES), I32)
    for t in range(TILES):
        for s in range(SIDES):
            spot = t * SIDES + s
            near, link = near_ref[t, s], link_ref[t, s]
            tile = jnp.where(near < 0, me * TILES, near)
            device = tile // TILES
            step = device // 2 - chip
            place = jnp.where(step == 0, 0, jnp.where((step == 1) == (chip % 2 == 0), 2, 4))
            place = place + (device % 2 != core).astype(I32)
            row = place * rows + (tile % TILES) * SIDES + link // 2
            out_ref[pl.ds(spot, channels, stride=SPOTS), :] = all_ref[pl.ds(row, channels, stride=SPOTS), :]
            turned = jnp.where(sub == spot, link % 2, turned)
            closed = jnp.where(sub == spot, (near < 0).astype(I32), closed)
    back = jnp.clip(TILE - 1 - lane, 0, LANES - 1)
    for k in range(channels):
        for h in range(0, SPOTS, 8):
            at = pl.ds(k * SPOTS + h, 8)
            values = out_ref[at, :]
            values = jnp.where(turned[h : h + 8] == 1, lane_gather(values, back[h : h + 8]), values)
            out_ref[at, :] = jnp.where((closed[h : h + 8] == 1) | (lane[h : h + 8] >= TILE), 0.0, values)


def spot_rows(ref, index):
    return ref[pl.ds(index * SPOTS, SPOTS), :]


def change_planes(own_ref, first_ref, second_ref, fixed_ref, tracers, scratch, lane, low):
    mix_a = spot_rows(fixed_ref, tracers) * spot_rows(first_ref, tracers)
    mix_b = spot_rows(fixed_ref, tracers + 1) * spot_rows(second_ref, tracers)
    for c in range(tracers):
        own = spot_rows(own_ref, c)
        change = own + mix_a * (spot_rows(first_ref, c) - own) + mix_b * (spot_rows(second_ref, c) - own)
        scratch[pl.ds(c * SPOTS, SPOTS), :] = change
    out = []
    for c in range(tracers):
        sides = [scratch[pl.ds(c * SPOTS + s, TILES, stride=SIDES), :] for s in range(SIDES)]
        sides = [jnp.concatenate([side, side], axis=0) for side in sides]
        west = jnp.where(low, pltpu.roll(sides[2], 63, 1), pltpu.roll(sides[2], 63 - FIRST_HIGH, 1))
        east = jnp.where(low, sides[3], pltpu.roll(sides[3], LANES - FIRST_HIGH, 1))
        out.append([sides[0], sides[1], jnp.where(lane < 63, east, west)])
    return out


def add_columns(planes, v, lane, low):
    x, y = cell_at(lane, low, v)
    west, east = x == 0, x == TILE - 1
    index = (y + jnp.where(west, 63, 0) - jnp.where(low, 0, FIRST_HIGH)) & (LANES - 1)
    edge = west | east
    return [jnp.where(edge, lane_gather(sides[2], index), 0.0) for sides in planes]


def add_rows(ref, planes, lane, low):
    place = (CELLS - TILE - HALF) % LANES
    for c, sides in enumerate(planes):
        ref[c, 0] = ref[c, 0] + jnp.where(low, sides[0], 0.0)
        turned = pltpu.roll(sides[1], place, 1)
        ref[c, COLS - 2] = ref[c, COLS - 2] + jnp.where(low | (lane < place), 0.0, turned)
        ref[c, COLS - 1] = ref[c, COLS - 1] + jnp.where(low | (lane >= place + TILE - LANES), 0.0, turned)


def write_to(ref, *lead):
    def write(v, row, part):
        ref[(*lead, v, pl.ds(row, TILES), slice(None))] = part

    return write


def open_kernel(
    adjoint_hbm, weights_hbm, vertical_hbm, mask_hbm, rate_hbm,
    pack_a, pack_b, edge_ref, wet_ref, mixing_ref, stay_ref, keep_ref,
    adjoint_ref, weights_ref, vertical_ref, mask_ref, rate_ref, lam_ref, spread, sems,
):
    tracers = lam_ref.shape[0]
    copies = [
        pltpu.make_async_copy(source, target, sems.at[i])
        for i, (source, target) in enumerate(
            (
                (mask_hbm, mask_ref),
                (weights_hbm, weights_ref),
                (vertical_hbm, vertical_ref),
                (adjoint_hbm, adjoint_ref),
                (rate_hbm, rate_ref),
            )
        )
    ]
    for copy in copies:
        copy.start()
    even = lax.axis_index("slab") % 2 == 0
    lane, low = position()
    copies[0].wait()
    fold(lambda a, n: mask_ref[0, :, a : a + n].astype(F32), write_to(wet_ref))
    copies[1].wait()
    fold(lambda a, n: weights_ref[0, :, a : a + n], write_to(mixing_ref))
    copies[2].wait()
    fold(lambda a, n: vertical_ref[0, :, a : a + n], write_to(stay_ref))
    copies[3].wait()
    for c in range(tracers):
        fold(lambda a, n, c=c: adjoint_ref[0, c, :, a : a + n], write_to(lam_ref, c))

    def start(v, carry):
        wet = wet_ref[v]
        mixing = wet * mixing_ref[v]
        mixing_ref[v] = mixing
        for c in range(tracers):
            spread[c, v + 1] = mixing * lam_ref[c, v]
        spread[tracers, v + 1] = wet
        vertical = stay_ref[v]
        pack_a[tracers, v] = wet * jnp.where(even, 1.0, vertical)
        pack_b[tracers, v] = wet * jnp.where(even, vertical, 1.0)
        return carry

    loop(start)
    for c in range(tracers + 1):
        set_guards(spread, c, low)
    for p, sides in enumerate(edge_sides(lambda p, v: spread[p, v + 1], tracers + 1, lane, low)):
        put_sides(edge_ref, p * SPOTS, sides)
    copies[4].wait()
    for c in range(tracers):
        fold(lambda a, n, c=c: 1.0 - rate_ref[c, :, a : a + n], write_to(keep_ref, c))

    def body(v, carry):
        x, _ = cell_at(lane, low, v)
        west, east = x == 0, x == TILE - 1
        wet = wet_ref[v]
        stay = 1.0 - mixing_ref[v] * inner_sum(spread, tracers, v, lane, west, east)
        stay_ref[v] = stay
        for c in range(tracers):
            moved = inner_sum(spread, c, v, lane, west, east)
            taken = (lam_ref[c, v] * stay + wet * moved) * keep_ref[c, v]
            pack_a[c, v] = taken
            pack_b[c, v] = taken
        return carry

    loop(body)


def fixed_kernel(keep_ref, pack_a, pack_b, out_ref):
    tracers = keep_ref.shape[0]
    lane, low = position()

    def load(p, v):
        return keep_ref[p, v] if p < tracers else (pack_a if p == tracers else pack_b)[tracers, v]

    for p, sides in enumerate(edge_sides(load, tracers + 2, lane, low)):
        put_sides(out_ref, p * SPOTS, sides)


def halo_kernel(near_ref, link_ref, all_ref, edge_ref, fixed_ref, out_a, out_b, wet_ref, halo_ref):
    channels = edge_ref.shape[0] // SPOTS
    tracers = channels - 1
    halos(near_ref, link_ref, all_ref, channels * SPOTS, channels, halo_ref)
    wet, halo_wet = spot_rows(edge_ref, tracers), spot_rows(halo_ref, tracers)
    wet_ref[pl.ds(0, SPOTS), :] = halo_wet
    wet_ref[pl.ds(SPOTS, SPOTS), :] = wet
    add_halos(halo_ref, edge_ref, fixed_ref, wet, halo_wet, tracers, out_a, out_b)


def halo_again_kernel(near_ref, link_ref, all_ref, edge_ref, fixed_ref, wet_ref, out_a, out_b, halo_ref):
    tracers = edge_ref.shape[0] // SPOTS
    halos(near_ref, link_ref, all_ref, tracers * SPOTS, tracers, halo_ref)
    add_halos(halo_ref, edge_ref, fixed_ref, spot_rows(wet_ref, 1), spot_rows(wet_ref, 0), tracers, out_a, out_b)


def add_halos(halo_ref, edge_ref, fixed_ref, wet, halo_wet, tracers, out_a, out_b):
    for c in range(tracers):
        change = spot_rows(fixed_ref, c) * (wet * spot_rows(halo_ref, c) - spot_rows(edge_ref, c) * halo_wet)
        for out in (out_a, out_b):
            out[pl.ds(c * SPOTS, SPOTS), :] = change
    out_a[pl.ds(tracers * SPOTS, SPOTS), :] = spot_rows(fixed_ref, tracers)
    out_b[pl.ds(tracers * SPOTS, SPOTS), :] = spot_rows(fixed_ref, tracers + 1)


def middle_kernel(
    change_ref, change_a, change_b, fixed_ref, pack_a, pack_b, from_a, from_b, wet_ref, mixing_ref, stay_ref, keep_ref,
    out_ref, edge_ref, mix_a_ref, mix_b_ref, lam_ref, spread, scratch,
):
    tracers = lam_ref.shape[0]
    lane, low = position()
    planes = change_planes(change_ref, change_a, change_b, fixed_ref, tracers, scratch, lane, low)

    def body(v, carry):
        first, second = pack_a[tracers, v] * from_a[tracers, v], pack_b[tracers, v] * from_b[tracers, v]
        mix_a_ref[v] = first
        mix_b_ref[v] = second
        extra = add_columns(planes, v, lane, low)
        for c in range(tracers):
            taken = pack_a[c, v]
            lam_ref[c, v] = taken + first * (from_a[c, v] - taken) + second * (from_b[c, v] - taken) + extra[c]
        return carry

    loop(body)
    add_rows(lam_ref, planes, lane, low)

    def spreads(v, carry):
        for c in range(tracers):
            spread[c, v + 1] = mixing_ref[v] * lam_ref[c, v]
        return carry

    loop(spreads)
    for c in range(tracers):
        set_guards(spread, c, low)
    for p, sides in enumerate(edge_sides(lambda p, v: spread[p, v + 1], tracers, lane, low)):
        put_sides(edge_ref, p * SPOTS, sides)

    def inner(v, carry):
        x, _ = cell_at(lane, low, v)
        west, east = x == 0, x == TILE - 1
        wet, stay = wet_ref[v], stay_ref[v]
        for c in range(tracers):
            moved = inner_sum(spread, c, v, lane, west, east)
            out_ref[c, v] = (lam_ref[c, v] * stay + wet * moved) * keep_ref[c, v]
        return carry

    loop(inner)


def close_kernel(
    owner_ref, change_ref, change_a, change_b, fixed_ref, taken_ref, from_a, from_b, mix_a_ref, mix_b_ref, wet_ref,
    state_ref, out_hbm, part_ref, lam_ref, term_ref, rows_ref, sums_ref, flat_ref, scratch, sems,
):
    tracers = taken_ref.shape[0]
    lane, low = position()
    planes = change_planes(change_ref, change_a, change_b, fixed_ref, tracers, scratch, lane, low)
    for c in range(tracers):
        fold(lambda a, n, c=c: state_ref[0, c, :, a : a + n], write_to(term_ref, c))

    def body(v, carry):
        first, second = mix_a_ref[v], mix_b_ref[v]
        extra = add_columns(planes, v, lane, low)
        for c in range(tracers):
            taken = taken_ref[c, v]
            lam_ref[c, v] = taken + first * (from_a[c, v] - taken) + second * (from_b[c, v] - taken) + extra[c]
        return carry

    loop(body)
    add_rows(lam_ref, planes, lane, low)

    def terms(v, carry):
        for c in range(tracers):
            term_ref[c, v] = wet_ref[v] * lam_ref[c, v] * term_ref[c, v]
        return carry

    loop(terms)
    copies = []
    for c in range(tracers):
        for v in range(COLS):
            values = lam_ref[c, v]
            flat_ref[0, c, :, v * LANES : (v + 1) * LANES] = values[:TILES]
            start = HALF + v * LANES
            width = min(LANES, CELLS - start)
            flat_ref[0, c, :, start : start + width] = values[TILES:, :width]
        copies.append(pltpu.make_async_copy(flat_ref.at[0, c], out_hbm.at[0, c], sems.at[c]))
        copies[-1].start()
    for c in range(tracers):
        guard = pltpu.roll(term_ref[c, 0], TILES, 0)
        for block in range(COARSE):
            total = [None, None]
            for y in range(block * BLOCK, (block + 1) * BLOCK):
                half = y * TILE // HALF
                v, shift = divmod(y * TILE - half * HALF, LANES)
                values = term_ref[c, v]
                if shift + TILE > LANES:
                    after = term_ref[c, v + 1] if v + 1 < COLS else guard
                    values = jnp.where(lane >= shift, values, after)
                if shift:
                    values = pltpu.roll(values, LANES - shift, 1)
                total[half] = values if total[half] is None else total[half] + values
            parts = [total[h][h * TILES : (h + 1) * TILES] for h in range(2) if total[h] is not None]
            summed = parts[0] if len(parts) == 1 else parts[0] + parts[1]
            summed = jnp.where(lane[:TILES] < TILE, summed, 0.0)
            rows_ref[pl.ds((c * COARSE + block) * TILES, TILES), :] = summed
    lane_in = lax.broadcasted_iota(I32, (LANES, LANES), 0)
    lane_out = lax.broadcasted_iota(I32, (LANES, LANES), 1)
    low_edge = lane_out * BLOCK
    pick = ((lane_in >= low_edge) & (lane_in < low_edge + BLOCK) & (lane_out < COARSE)).astype(F32)
    sums_ref[...] = jnp.dot(rows_ref[...], pick, precision=lax.Precision.HIGHEST, preferred_element_type=F32)
    for spot in range(8):
        total = jnp.zeros((TILES, LANES), F32)
        for k in range(tracers * COARSE):
            start = k * COARSE - spot * LANES
            if start >= LANES or start + COARSE <= 0:
                continue
            values = sums_ref[pl.ds(k * TILES, TILES), :]
            values = pltpu.roll(values, start % LANES, 1) if start % LANES else values
            if start < 0:
                values = jnp.where(lane[:TILES] < start + COARSE, values, 0.0)
            elif start + COARSE > LANES:
                values = jnp.where(lane[:TILES] >= start, values, 0.0)
            total = total + values
        rows_ref[pl.ds(spot, TILES, stride=8), :] = total
    part_ref[...] = jnp.zeros_like(part_ref)
    me = lax.axis_index("tiles")
    for t in range(TILES):
        owner = owner_ref[me * TILES + t]
        part_ref[owner] = part_ref[owner] + rows_ref[pl.ds(t * 8, 8), :]
    for copy in copies:
        copy.wait()


def swaps(count, width=1):
    found = []
    for first in (0, 1):
        found.append(
            [
                pair
                for i in range(first, count // width - 1, 2)
                for k in range(width)
                for pair in ((i * width + k, (i + 1) * width + k), ((i + 1) * width + k, i * width + k))
            ]
        )
    return found


VMEM, SMEM, HBM = (pl.BlockSpec(memory_space=space) for space in (pltpu.VMEM, pltpu.SMEM, pltpu.HBM))


def call(kernel, ins, out, scratch, outs=None):
    return pl.pallas_call(
        kernel,
        out_shape=[jax.ShapeDtypeStruct(shape, F32) for shape in out],
        in_specs=ins,
        out_specs=outs or [VMEM] * len(out),
        scratch_shapes=[pltpu.VMEM(shape, F32) if isinstance(shape, tuple) else shape for shape in scratch],
        compiler_params=pltpu.CompilerParams(vmem_limit_bytes=32 * 1024 * 1024),
        name=kernel.__name__,
    )


def shards(adjoint, state, weights, vertical, mask, rate, neighbours, links, owners):
    tracers = adjoint.shape[1]
    number = lax.axis_size("tiles")
    even_swap, odd_swap = swaps(lax.axis_size("slab"))
    core_swap = swaps(2)[0]
    core_swap = [(2 * i + a, 2 * i + b) for i in range(number // 2) for a, b in core_swap]
    even_chips, odd_chips = swaps(number, 2)
    plane = (COLS, 8, LANES)
    planes = (tracers, *plane)
    pack = (tracers + 1, *plane)
    guarded = (COLS + 2, 8, LANES)
    rows = tracers * SPOTS

    def around(edge):
        both = jnp.concatenate([edge, lax.ppermute(edge, "tiles", core_swap)])
        return jnp.concatenate(
            [both, lax.ppermute(both, "tiles", even_chips), lax.ppermute(both, "tiles", odd_chips)]
        )

    def across(first, second):
        return lax.ppermute(first, "slab", even_swap), lax.ppermute(second, "slab", odd_swap)

    pack_a, pack_b, edge, wet, mixing, stay, keep = call(
        open_kernel,
        [HBM] * 5,
        [pack, pack, (rows + SPOTS, LANES), plane, plane, plane, planes],
        [adjoint.shape, weights.shape, vertical.shape, pltpu.VMEM(mask.shape, I32), rate.shape, planes]
        + [(tracers + 1, *guarded), pltpu.SemaphoreType.DMA((5,))],
    )(*(pltpu.with_memory_space_constraint(x, pltpu.HBM) for x in (adjoint, weights, vertical, mask, rate)))
    from_a, from_b = across(pack_a, pack_b)
    near = around(edge)
    (fixed,) = call(fixed_kernel, [VMEM] * 3, [((tracers + 2) * SPOTS, LANES)], [])(keep, pack_a, pack_b)
    change_a, change_b, edge_wet = call(
        halo_kernel,
        [SMEM] * 2 + [VMEM] * 3,
        [(rows + SPOTS, LANES)] * 2 + [(2 * SPOTS, LANES)],
        [(rows + SPOTS, LANES)],
    )(neighbours, links, near, edge, fixed)
    got_a, got_b = across(change_a, change_b)
    taken, edge, mix_a, mix_b = call(
        middle_kernel,
        [VMEM] * 12,
        [planes, (rows, LANES), plane, plane],
        [planes, (tracers, *guarded), (rows, LANES)],
    )(change_a, got_a, got_b, fixed, pack_a, pack_b, from_a, from_b, wet, mixing, stay, keep)
    from_a, from_b = across(taken, taken)
    near = around(edge)
    change_a, change_b = call(
        halo_again_kernel, [SMEM] * 2 + [VMEM] * 4, [(rows + SPOTS, LANES)] * 2, [(rows, LANES)]
    )(neighbours, links, near, edge, fixed, edge_wet)
    got_a, got_b = across(change_a, change_b)
    sums = (tracers * COARSE * TILES + 4, LANES)
    out, part = call(
        close_kernel,
        [SMEM] + [VMEM] * 11,
        [adjoint.shape, (number, 8, LANES)],
        [planes, planes, sums, sums, adjoint.shape, (rows, LANES), pltpu.SemaphoreType.DMA((tracers,))],
        [HBM, VMEM],
    )(owners, change_a, got_a, got_b, fixed, taken, from_a, from_b, mix_a, mix_b, wet, state)
    part = lax.all_to_all(part, "tiles", 0, 0, tiled=True)
    gradient = part.sum(axis=0).reshape(1, 1, 8 * LANES)[:, :, : tracers * COARSE * COARSE]
    return out, gradient


def solution(mesh):
    placed = (
        P("slab", None, "tiles", None),
        P("slab", None, "tiles", None),
        P("slab", "tiles", None),
        P("slab", "tiles", None),
        P("slab", "tiles", None),
        P(None, "tiles", None),
        P("tiles", None),
        P("tiles", None),
        P(),
    )
    return jax.shard_map(
        shards,
        mesh=mesh,
        in_specs=placed,
        out_specs=(P("slab", None, "tiles", None), P("slab", "tiles", None)),
        check_vma=False,
    )
```

```python
import functools

import jax
import jax.numpy as jnp
from jax import lax
from jax.experimental import pallas as pl
from jax.experimental.pallas import tpu as pltpu
from jax.sharding import PartitionSpec as P

TILE = 90
CELLS = TILE * TILE
SUBSTEPS = 2
BLOCK = 6
COARSE = 15
LANES = 128
COLS = 32
HALF = COLS * LANES
TILES = 4
SIDES = 4
SPOTS = TILES * SIDES
CHANNELS = 4
ROWS = SPOTS * CHANNELS
SHOWN = ROWS + 2 * SIDES * CHANNELS
FIRST_HIGH = HALF // TILE
UNROLL = 8
F32 = jnp.float32
I32 = jnp.int32


def position():
    lane = lax.broadcasted_iota(I32, (8, LANES), 1)
    low = lax.broadcasted_iota(I32, (8, LANES), 0) < TILES
    return lane, low


def cell_at(lane, low, v):
    cell = lane + jnp.where(low, 0, HALF) + v * LANES
    y = (cell * 46604) >> 22
    return cell - y * TILE, y


def lane_gather(values, index):
    return jnp.take_along_axis(values, index, axis=1, mode="promise_in_bounds")


def loop(body, carry=0):
    return lax.fori_loop(0, COLS, body, carry, unroll=UNROLL)


def fold(read, write):
    for v in range(COLS):
        write(v, 0, read(v * LANES, LANES))
        start = HALF + v * LANES
        width = min(LANES, CELLS - start)
        part = read(start, width)
        if width < LANES:
            part = jnp.concatenate([part, jnp.zeros((TILES, LANES - width), F32)], axis=1)
        write(v, TILES, part)


def set_guards(ref, plane, low):
    first, last = ref[plane, 1], ref[plane, COLS]
    ref[plane, 0] = jnp.where(low, 0.0, pltpu.roll(last, TILES, 0))
    ref[plane, COLS + 1] = jnp.where(low, pltpu.roll(first, TILES, 0), 0.0)


def inner_sum(ref, plane, v, lane, west, east):
    before, here, after = ref[plane, v], ref[plane, v + 1], ref[plane, v + 2]
    left = pltpu.roll(jnp.where(lane < LANES - 1, here, before), 1, 1)
    right = pltpu.roll(jnp.where(lane >= 1, here, after), LANES - 1, 1)
    up = pltpu.roll(jnp.where(lane < LANES - TILE, here, before), TILE, 1)
    down = pltpu.roll(jnp.where(lane >= TILE, here, after), LANES - TILE, 1)
    return jnp.where(west, 0.0, left) + jnp.where(east, 0.0, right) + (up + down)


def edge_sides(load, planes, lane, low):
    step = lane & 63
    base = TILE * step + jnp.where(low, 0, FIRST_HIGH * TILE - HALF) + jnp.where(lane < 64, TILE - 1, TILE)
    index, column = base & (LANES - 1), base >> 7

    def body(v, found):
        hit = column == v
        return tuple(jnp.where(hit, lane_gather(load(p, v), index), found[p]) for p in range(planes))

    found = loop(body, tuple(jnp.zeros((8, LANES), F32) for _ in range(planes)))
    bottom = CELLS - TILE - HALF + lane
    edge = lane < TILE
    first_low = jnp.where(low, lane + 63, lane - FIRST_HIGH + 63) & (LANES - 1)
    last_low = jnp.where(low, lane, lane - FIRST_HIGH) & (LANES - 1)
    out = []
    for p in range(planes):
        top = load(p, 0)
        picked = jnp.where(
            (bottom >> 7) == COLS - 2,
            lane_gather(load(p, COLS - 2), bottom & (LANES - 1)),
            lane_gather(load(p, COLS - 1), bottom & (LANES - 1)),
        )
        west, east = lane_gather(found[p], first_low), lane_gather(found[p], last_low)
        west = jnp.where(low, jnp.where(lane == 0, top, west), west)
        west_low, east_low = west[:TILES], east[:TILES]
        here = lane[:TILES]
        west = jnp.where(here <= FIRST_HIGH, west_low, west[TILES:])
        east = jnp.where(here < FIRST_HIGH, east_low, east[TILES:])
        inside = here < TILE
        out.append(
            [
                jnp.where(inside, top[:TILES], 0.0),
                jnp.where(inside, picked[TILES:], 0.0),
                jnp.where(inside, west, 0.0),
                jnp.where(inside, east, 0.0),
            ]
        )
    return out


def put_sides(ref, channel, sides):
    for s in range(SIDES):
        ref[pl.ds(s * CHANNELS + channel, TILES, stride=SIDES * CHANNELS), :] = sides[s]


def channel_rows(ref, channel):
    return ref[pl.ds(channel, SPOTS, stride=CHANNELS), :]


def halos(near_ref, link_ref, all_ref, out_ref):
    me = lax.axis_index("tiles")
    chip, core = me // 2, me % 2
    even = chip % 2 == 0
    turned, closed = [], []
    for t in range(TILES):
        for s in range(SIDES):
            near, link = near_ref[t, s], link_ref[t, s]
            tile = jnp.where(near < 0, me * TILES, near)
            device = tile // TILES
            inner = tile % TILES
            step = device // 2 - chip
            place = jnp.where(step == 0, 0, jnp.where((step == 1) == even, 2 * SHOWN, SHOWN))
            far = jnp.where(inner == 0, ROWS, ROWS + SIDES * CHANNELS)
            row = place + jnp.where(device % 2 == core, inner * (SIDES * CHANNELS), far) + (link // 2) * CHANNELS
            out_ref[pl.ds((t * SIDES + s) * CHANNELS, CHANNELS), :] = all_ref[pl.ds(row, CHANNELS), :]
            turned.append(link % 2)
            closed.append((near < 0).astype(I32))
    lane, low = position()
    back = jnp.clip(TILE - 1 - lane, 0, LANES - 1)
    for k in range(0, SPOTS, 2):
        at = pl.ds(k * CHANNELS, 8)
        values = out_ref[at, :]
        values = jnp.where(jnp.where(low, turned[k], turned[k + 1]) == 1, lane_gather(values, back), values)
        shut = jnp.where(low, closed[k], closed[k + 1]) == 1
        out_ref[at, :] = jnp.where(shut | (lane >= TILE), 0.0, values)


def change_planes(own_a, own_b, got_a, got_b, tracers, scratch, lane, low):
    mix_a = channel_rows(own_a, tracers) * channel_rows(got_a, tracers)
    mix_b = channel_rows(own_b, tracers) * channel_rows(got_b, tracers)
    for c in range(tracers):
        own = channel_rows(own_a, c)
        scratch[pl.ds(c * SPOTS, SPOTS), :] = (
            own + mix_a * (channel_rows(got_a, c) - own) + mix_b * (channel_rows(got_b, c) - own)
        )
    out = []
    for c in range(tracers):
        sides = [scratch[pl.ds(c * SPOTS + s, TILES, stride=SIDES), :] for s in range(SIDES)]
        sides = [jnp.concatenate([side, side], axis=0) for side in sides]
        west = jnp.where(low, pltpu.roll(sides[2], 63, 1), pltpu.roll(sides[2], 63 - FIRST_HIGH, 1))
        east = jnp.where(low, sides[3], pltpu.roll(sides[3], LANES - FIRST_HIGH, 1))
        out.append([sides[0], sides[1], jnp.where(lane < 63, east, west)])
    return out


def add_columns(planes, v, lane, low):
    x, y = cell_at(lane, low, v)
    west, east = x == 0, x == TILE - 1
    index = (y + jnp.where(west, 63, 0) - jnp.where(low, 0, FIRST_HIGH)) & (LANES - 1)
    edge = west | east
    return [jnp.where(edge, lane_gather(sides[2], index), 0.0) for sides in planes]


def add_rows(ref, planes, lane, low):
    place = (CELLS - TILE - HALF) % LANES
    for c, sides in enumerate(planes):
        ref[c, 0] = ref[c, 0] + jnp.where(low, sides[0], 0.0)
        turned = pltpu.roll(sides[1], place, 1)
        ref[c, COLS - 2] = ref[c, COLS - 2] + jnp.where(low | (lane < place), 0.0, turned)
        ref[c, COLS - 1] = ref[c, COLS - 1] + jnp.where(low | (lane >= place + TILE - LANES), 0.0, turned)


def write_to(ref, *lead):
    def write(v, row, part):
        ref[(*lead, v, pl.ds(row, TILES), slice(None))] = part

    return write


def open_kernel(
    adjoint_hbm, weights_hbm, mask_hbm, near_hbm, link_hbm,
    edge_ref, lam_ref, wet_ref, mixing_ref, spread, near_ref, link_ref,
    adjoint_ref, weights_ref, mask_ref, sems,
):
    tracers = lam_ref.shape[0]
    pairs = (
        (mask_hbm, mask_ref),
        (weights_hbm, weights_ref),
        (adjoint_hbm, adjoint_ref),
        (near_hbm, near_ref),
        (link_hbm, link_ref),
    )
    copies = [pltpu.make_async_copy(source, target, sems.at[i]) for i, (source, target) in enumerate(pairs)]
    for copy in copies:
        copy.start()
    lane, low = position()
    copies[0].wait()
    fold(lambda a, n: mask_ref[0, :, a : a + n].astype(F32), write_to(wet_ref))
    copies[1].wait()
    fold(lambda a, n: weights_ref[0, :, a : a + n], write_to(mixing_ref))
    copies[2].wait()
    for c in range(tracers):
        fold(lambda a, n, c=c: adjoint_ref[0, c, :, a : a + n], write_to(lam_ref, c))

    def start(v, carry):
        wet = wet_ref[v]
        mixing = wet * mixing_ref[v]
        mixing_ref[v] = mixing
        for c in range(tracers):
            spread[c, v + 1] = mixing * lam_ref[c, v]
        spread[tracers, v + 1] = wet
        return carry

    loop(start)
    for c in range(tracers + 1):
        set_guards(spread, c, low)
    for p, sides in enumerate(edge_sides(lambda p, v: spread[p, v + 1], tracers + 1, lane, low)):
        put_sides(edge_ref, p, sides)
    copies[3].wait()
    copies[4].wait()


def inner_first_kernel(spread, lam_ref, wet_ref, mixing_ref, vertical_ref, rate_ref, pack_a, pack_b, stay_ref, keep_ref):
    tracers = lam_ref.shape[0]
    even = lax.axis_index("slab") % 2 == 0
    lane, low = position()
    fold(lambda a, n: vertical_ref[0, :, a : a + n], write_to(stay_ref))
    for c in range(tracers):
        fold(lambda a, n, c=c: 1.0 - rate_ref[c, :, a : a + n], write_to(keep_ref, c))

    def body(v, carry):
        x, _ = cell_at(lane, low, v)
        west, east = x == 0, x == TILE - 1
        wet, vertical = wet_ref[v], stay_ref[v]
        pack_a[tracers, v] = wet * jnp.where(even, 1.0, vertical)
        pack_b[tracers, v] = wet * jnp.where(even, vertical, 1.0)
        stay = 1.0 - mixing_ref[v] * inner_sum(spread, tracers, v, lane, west, east)
        stay_ref[v] = stay
        for c in range(tracers):
            moved = inner_sum(spread, c, v, lane, west, east)
            taken = (lam_ref[c, v] * stay + wet * moved) * keep_ref[c, v]
            pack_a[c, v] = taken
            pack_b[c, v] = taken
        return carry

    loop(body)


def inner_kernel(spread, lam_ref, wet_ref, stay_ref, keep_ref, out_ref):
    tracers = lam_ref.shape[0]
    lane, low = position()

    def body(v, carry):
        x, _ = cell_at(lane, low, v)
        west, east = x == 0, x == TILE - 1
        wet, stay = wet_ref[v], stay_ref[v]
        for c in range(tracers):
            moved = inner_sum(spread, c, v, lane, west, east)
            out_ref[c, v] = (lam_ref[c, v] * stay + wet * moved) * keep_ref[c, v]
        return carry

    loop(body)


def fixed_kernel(keep_ref, pack_a, pack_b, out_a, out_b):
    tracers = keep_ref.shape[0]
    lane, low = position()

    def load(p, v):
        return keep_ref[p, v] if p < tracers else (pack_a if p == tracers else pack_b)[tracers, v]

    found = edge_sides(load, tracers + 2, lane, low)
    for c in range(tracers):
        put_sides(out_a, c, found[c])
        put_sides(out_b, c, found[c])
    put_sides(out_a, tracers, found[tracers])
    put_sides(out_b, tracers, found[tracers + 1])


def halo_kernel(near_ref, link_ref, all_ref, edge_ref, fixed_a, fixed_b, out_a, out_b, halo_ref):
    tracers = CHANNELS - 1
    halos(near_ref, link_ref, all_ref, halo_ref)
    wet, halo_wet = channel_rows(edge_ref, tracers), channel_rows(halo_ref, tracers)
    for c in range(tracers):
        change = channel_rows(fixed_a, c) * (wet * channel_rows(halo_ref, c) - channel_rows(edge_ref, c) * halo_wet)
        for out in (out_a, out_b):
            out[pl.ds(c, SPOTS, stride=CHANNELS), :] = change
    out_a[pl.ds(tracers, SPOTS, stride=CHANNELS), :] = channel_rows(fixed_a, tracers)
    out_b[pl.ds(tracers, SPOTS, stride=CHANNELS), :] = channel_rows(fixed_b, tracers)


def mix_first_kernel(pack_a, pack_b, from_a, from_b, lam_ref, mix_a_ref, mix_b_ref):
    tracers = lam_ref.shape[0]

    def body(v, carry):
        first, second = pack_a[tracers, v] * from_a[tracers, v], pack_b[tracers, v] * from_b[tracers, v]
        mix_a_ref[v] = first
        mix_b_ref[v] = second
        for c in range(tracers):
            taken = pack_a[c, v]
            lam_ref[c, v] = taken + first * (from_a[c, v] - taken) + second * (from_b[c, v] - taken)
        return carry

    loop(body)


def mix_kernel(taken_ref, from_a, from_b, mix_a_ref, mix_b_ref, wet_ref, state_ref, lam_ref, term_ref):
    tracers = lam_ref.shape[0]
    for c in range(tracers):
        fold(lambda a, n, c=c: state_ref[0, c, :, a : a + n], write_to(term_ref, c))

    def body(v, carry):
        first, second, wet = mix_a_ref[v], mix_b_ref[v], wet_ref[v]
        for c in range(tracers):
            taken = taken_ref[c, v]
            lam_ref[c, v] = taken + first * (from_a[c, v] - taken) + second * (from_b[c, v] - taken)
            term_ref[c, v] = wet * term_ref[c, v]
        return carry

    loop(body)


def middle_kernel(
    change_a, change_b, got_a, got_b, before_ref, mixing_ref, wet_edge_ref, edge_ref, lam_ref, spread, scratch
):
    tracers = lam_ref.shape[0]
    lane, low = position()
    planes = change_planes(change_a, change_b, got_a, got_b, tracers, scratch, lane, low)

    def body(v, carry):
        extra = add_columns(planes, v, lane, low)
        mixing = mixing_ref[v]
        for c in range(tracers):
            lam = before_ref[c, v] + extra[c]
            lam_ref[c, v] = lam
            spread[c, v + 1] = mixing * lam
        return carry

    loop(body)
    add_rows(lam_ref, planes, lane, low)
    for c in range(tracers):
        for v in (0, COLS - 2, COLS - 1):
            spread[c, v + 1] = mixing_ref[v] * lam_ref[c, v]
        set_guards(spread, c, low)
    for p, sides in enumerate(edge_sides(lambda p, v: spread[p, v + 1], tracers, lane, low)):
        put_sides(edge_ref, p, sides)
    edge_ref[pl.ds(tracers, SPOTS, stride=CHANNELS), :] = channel_rows(wet_edge_ref, tracers)


def close_kernel(
    owner_hbm, change_a, change_b, got_a, got_b, before_ref, weighted_ref,
    out_hbm, part_ref, lam_ref, term_ref, rows_ref, sums_ref, flat_ref, scratch, owner_ref, sems,
):
    tracers = lam_ref.shape[0]
    owner_copy = pltpu.make_async_copy(owner_hbm, owner_ref, sems.at[tracers])
    owner_copy.start()
    lane, low = position()
    planes = change_planes(change_a, change_b, got_a, got_b, tracers, scratch, lane, low)

    def body(v, carry):
        extra = add_columns(planes, v, lane, low)
        for c in range(tracers):
            lam = before_ref[c, v] + extra[c]
            lam_ref[c, v] = lam
            term_ref[c, v] = weighted_ref[c, v] * lam
        return carry

    loop(body)
    add_rows(lam_ref, planes, lane, low)
    for c in range(tracers):
        for v in (0, COLS - 2, COLS - 1):
            term_ref[c, v] = weighted_ref[c, v] * lam_ref[c, v]
    copies = []
    for c in range(tracers):
        for v in range(COLS):
            values = lam_ref[c, v]
            flat_ref[0, c, :, v * LANES : (v + 1) * LANES] = values[:TILES]
            start = HALF + v * LANES
            width = min(LANES, CELLS - start)
            flat_ref[0, c, :, start : start + width] = values[TILES:, :width]
        copies.append(pltpu.make_async_copy(flat_ref.at[0, c], out_hbm.at[0, c], sems.at[c]))
        copies[-1].start()
    for c in range(tracers):
        guard = pltpu.roll(term_ref[c, 0], TILES, 0)
        for block in range(COARSE):
            total = [None, None]
            for y in range(block * BLOCK, (block + 1) * BLOCK):
                half = y * TILE // HALF
                v, shift = divmod(y * TILE - half * HALF, LANES)
                values = term_ref[c, v]
                if shift + TILE > LANES:
                    after = term_ref[c, v + 1] if v + 1 < COLS else guard
                    values = jnp.where(lane >= shift, values, after)
                if shift:
                    values = pltpu.roll(values, LANES - shift, 1)
                total[half] = values if total[half] is None else total[half] + values
            parts = [total[h][h * TILES : (h + 1) * TILES] for h in range(2) if total[h] is not None]
            summed = parts[0] if len(parts) == 1 else parts[0] + parts[1]
            summed = jnp.where(lane[:TILES] < TILE, summed, 0.0)
            rows_ref[pl.ds((c * COARSE + block) * TILES, TILES), :] = summed
    lane_in = lax.broadcasted_iota(I32, (LANES, LANES), 0)
    lane_out = lax.broadcasted_iota(I32, (LANES, LANES), 1)
    low_edge = lane_out * BLOCK
    pick = ((lane_in >= low_edge) & (lane_in < low_edge + BLOCK) & (lane_out < COARSE)).astype(F32)
    sums_ref[...] = jnp.dot(rows_ref[...], pick, precision=lax.Precision.HIGHEST, preferred_element_type=F32)
    for spot in range(8):
        total = jnp.zeros((TILES, LANES), F32)
        for k in range(tracers * COARSE):
            start = k * COARSE - spot * LANES
            if start >= LANES or start + COARSE <= 0:
                continue
            values = sums_ref[pl.ds(k * TILES, TILES), :]
            values = pltpu.roll(values, start % LANES, 1) if start % LANES else values
            if start < 0:
                values = jnp.where(lane[:TILES] < start + COARSE, values, 0.0)
            elif start + COARSE > LANES:
                values = jnp.where(lane[:TILES] >= start, values, 0.0)
            total = total + values
        rows_ref[pl.ds(spot, TILES, stride=8), :] = total
    part_ref[...] = jnp.zeros_like(part_ref)
    me = lax.axis_index("tiles")
    owner_copy.wait()
    for t in range(TILES):
        owner = owner_ref[me * TILES + t]
        part_ref[owner] = part_ref[owner] + rows_ref[pl.ds(t * 8, 8), :]
    for copy in copies:
        copy.wait()


def swaps(count, width=1):
    found = []
    for first in (0, 1):
        found.append(
            [
                pair
                for i in range(first, count // width - 1, 2)
                for k in range(width)
                for pair in ((i * width + k, (i + 1) * width + k), ((i + 1) * width + k, i * width + k))
            ]
        )
    return found


VMEM, SMEM, HBM = (pl.BlockSpec(memory_space=space) for space in (pltpu.VMEM, pltpu.SMEM, pltpu.HBM))


def call(kernel, ins, out, scratch, outs=None):
    return pl.pallas_call(
        kernel,
        out_shape=[jax.ShapeDtypeStruct(shape, F32) if isinstance(shape, tuple) else shape for shape in out],
        in_specs=ins,
        out_specs=outs or [VMEM] * len(out),
        scratch_shapes=[pltpu.VMEM(shape, F32) if isinstance(shape, tuple) else shape for shape in scratch],
        compiler_params=pltpu.CompilerParams(vmem_limit_bytes=32 * 1024 * 1024),
        name=kernel.__name__,
    )


def shards(adjoint, state, weights, vertical, mask, rate, neighbours, links, owners):
    tracers = adjoint.shape[1]
    number = lax.axis_size("tiles")
    even_swap, odd_swap = swaps(lax.axis_size("slab"))
    core_swap = [(2 * i + a, 2 * i + 1 - a) for i in range(number // 2) for a in range(2)]
    even_chips, odd_chips = swaps(number, 2)
    passing = swaps(number, 4)[0]
    plane = (COLS, 8, LANES)
    planes = (tracers, *plane)
    pack = (tracers + 1, *plane)
    guarded = (COLS + 2, 8, LANES)
    edges = (ROWS, LANES)
    block = SIDES * CHANNELS

    def around(edge, other):
        shown = jnp.concatenate([edge, other[:block], other[ROWS - block :]])
        even = lax.ppermute(shown, "tiles", even_chips)
        if number == 8:
            odd = lax.ppermute(even, "tiles", passing)
        else:
            odd = lax.ppermute(shown, "tiles", odd_chips)
        return jnp.concatenate([shown, odd, even])

    def across(first, second):
        return lax.ppermute(first, "slab", even_swap), lax.ppermute(second, "slab", odd_swap)

    table = jax.ShapeDtypeStruct(neighbours.shape, I32)
    edge, lam, wet, mixing, spread, neighbours, links = call(
        open_kernel,
        [HBM] * 5,
        [edges, planes, plane, plane, (tracers + 1, *guarded), table, table],
        [adjoint.shape, weights.shape, pltpu.VMEM(mask.shape, I32), pltpu.SemaphoreType.DMA((5,))],
    )(*(pltpu.with_memory_space_constraint(x, pltpu.HBM) for x in (adjoint, weights, mask, neighbours, links)))
    other = lax.ppermute(edge, "tiles", core_swap)
    pack_a, pack_b, stay, keep = call(inner_first_kernel, [VMEM] * 6, [pack, pack, plane, planes], [])(
        spread, lam, wet, mixing, vertical, rate
    )
    pack_a, pack_b, other = lax.optimization_barrier((pack_a, pack_b, other))
    from_a, from_b = across(pack_a, pack_b)
    near = around(edge, other)
    fixed_a, fixed_b = call(fixed_kernel, [VMEM] * 3, [edges] * 2, [])(keep, pack_a, pack_b)
    halo = call(halo_kernel, [SMEM] * 2 + [VMEM] * 4, [edges] * 2, [edges])
    change_a, change_b = halo(neighbours, links, near, edge, fixed_a, fixed_b)
    got_a, got_b = across(change_a, change_b)
    before, mix_a, mix_b = call(mix_first_kernel, [VMEM] * 4, [planes, plane, plane], [])(
        pack_a, pack_b, from_a, from_b
    )
    edge, lam, spread = call(middle_kernel, [VMEM] * 7, [edges, planes, (tracers, *guarded)], [edges])(
        change_a, change_b, got_a, got_b, before, mixing, edge
    )
    other = lax.ppermute(edge, "tiles", core_swap)
    (taken,) = call(inner_kernel, [VMEM] * 5, [planes], [])(spread, lam, wet, stay, keep)
    taken, other = lax.optimization_barrier((taken, other))
    from_a, from_b = across(taken, taken)
    near = around(edge, other)
    change_a, change_b = halo(neighbours, links, near, edge, fixed_a, fixed_b)
    got_a, got_b = across(change_a, change_b)
    before, weighted = call(mix_kernel, [VMEM] * 7, [planes, planes], [])(
        taken, from_a, from_b, mix_a, mix_b, wet, state
    )
    sums = (tracers * COARSE * TILES + 4, LANES)
    out, part = call(
        close_kernel,
        [HBM] + [VMEM] * 6,
        [adjoint.shape, (number, 8, LANES)],
        [planes, planes, sums, sums, adjoint.shape, edges]
        + [pltpu.SMEM(owners.shape, I32), pltpu.SemaphoreType.DMA((tracers + 1,))],
        [HBM, VMEM],
    )(pltpu.with_memory_space_constraint(owners, pltpu.HBM), change_a, change_b, got_a, got_b, before, weighted)
    part = lax.all_to_all(part, "tiles", 0, 0, tiled=True)
    gradient = part.sum(axis=0).reshape(1, 1, 8 * LANES)[:, :, : tracers * COARSE * COARSE]
    return out, gradient


def solution(mesh):
    placed = (
        P("slab", None, "tiles", None),
        P("slab", None, "tiles", None),
        P("slab", "tiles", None),
        P("slab", "tiles", None),
        P("slab", "tiles", None),
        P(None, "tiles", None),
        P("tiles", None),
        P("tiles", None),
        P(),
    )
    return jax.shard_map(
        shards,
        mesh=mesh,
        in_specs=placed,
        out_specs=(P("slab", None, "tiles", None), P("slab", "tiles", None)),
        check_vma=False,
    )
```

```python
import functools

import jax
import jax.numpy as jnp
from jax import lax
from jax.experimental import pallas as pl
from jax.experimental.pallas import tpu as pltpu
from jax.sharding import PartitionSpec as P

TILE = 90
CELLS = TILE * TILE
SUBSTEPS = 2
BLOCK = 6
COARSE = 15
LANES = 128
COLS = 32
HALF = COLS * LANES
TILES = 4
SIDES = 4
SPOTS = TILES * SIDES
CHANNELS = 4
ROWS = SPOTS * CHANNELS
TILE_ROWS = SIDES * CHANNELS
SHOWN = ROWS + TILE_ROWS
OWN = 0 + SHOWN
ODD = 0 + SHOWN + SHOWN
EVEN = 0
OTHER = 0 + SHOWN + SHOWN + SHOWN
CLOSED = -8
TURNED = 1 << 16
FIRST_HIGH = HALF // TILE
UNROLL = 32
F32 = jnp.float32
I32 = jnp.int32


def position():
    lane = lax.broadcasted_iota(I32, (8, LANES), 1)
    low = lax.broadcasted_iota(I32, (8, LANES), 0) < TILES
    return lane, low


def cell_at(lane, low, v):
    cell = lane + jnp.where(low, 0, HALF) + v * LANES
    y = (cell * 46604) >> 22
    return cell - y * TILE, y


def lane_gather(values, index):
    return jnp.take_along_axis(values, index, axis=1, mode="promise_in_bounds")


def loop(body, carry=0):
    return lax.fori_loop(0, COLS, body, carry, unroll=UNROLL)


def fold(read, write):
    for v in range(COLS):
        write(v, 0, read(v * LANES, LANES))
        start = HALF + v * LANES
        width = min(LANES, CELLS - start)
        part = read(start, width)
        if width < LANES:
            part = jnp.concatenate([part, jnp.zeros((TILES, LANES - width), F32)], axis=1)
        write(v, TILES, part)


def set_guards(ref, plane, low):
    first, last = ref[plane, 1], ref[plane, COLS]
    ref[plane, 0] = jnp.where(low, 0.0, pltpu.roll(last, TILES, 0))
    ref[plane, COLS + 1] = jnp.where(low, pltpu.roll(first, TILES, 0), 0.0)


def inner_sum(ref, plane, v, lane, west, east):
    before, here, after = ref[plane, v], ref[plane, v + 1], ref[plane, v + 2]
    left = pltpu.roll(jnp.where(lane < LANES - 1, here, before), 1, 1)
    right = pltpu.roll(jnp.where(lane >= 1, here, after), LANES - 1, 1)
    up = pltpu.roll(jnp.where(lane < LANES - TILE, here, before), TILE, 1)
    down = pltpu.roll(jnp.where(lane >= TILE, here, after), LANES - TILE, 1)
    return jnp.where(west, 0.0, left) + jnp.where(east, 0.0, right) + (up + down)


def edge_sides(load, planes, lane, low):
    step = lane & 63
    base = TILE * step + jnp.where(low, 0, FIRST_HIGH * TILE - HALF) + jnp.where(lane < 64, TILE - 1, TILE)
    index, column = base & (LANES - 1), base >> 7

    def body(v, found):
        hit = column == v
        return tuple(jnp.where(hit, lane_gather(load(p, v), index), found[p]) for p in range(planes))

    found = loop(body, tuple(jnp.zeros((8, LANES), F32) for _ in range(planes)))
    bottom = CELLS - TILE - HALF + lane
    edge = lane < TILE
    first_low = jnp.where(low, lane + 63, lane - FIRST_HIGH + 63) & (LANES - 1)
    last_low = jnp.where(low, lane, lane - FIRST_HIGH) & (LANES - 1)
    out = []
    for p in range(planes):
        top = load(p, 0)
        picked = jnp.where(
            (bottom >> 7) == COLS - 2,
            lane_gather(load(p, COLS - 2), bottom & (LANES - 1)),
            lane_gather(load(p, COLS - 1), bottom & (LANES - 1)),
        )
        west, east = lane_gather(found[p], first_low), lane_gather(found[p], last_low)
        west = jnp.where(low, jnp.where(lane == 0, top, west), west)
        west_low, east_low = west[:TILES], east[:TILES]
        here = lane[:TILES]
        west = jnp.where(here <= FIRST_HIGH, west_low, west[TILES:])
        east = jnp.where(here < FIRST_HIGH, east_low, east[TILES:])
        inside = here < TILE
        out.append(
            [
                jnp.where(inside, top[:TILES], 0.0),
                jnp.where(inside, picked[TILES:], 0.0),
                jnp.where(inside, west, 0.0),
                jnp.where(inside, east, 0.0),
            ]
        )
    return out


def put_sides(ref, channel, sides):
    for s in range(SIDES):
        ref[pl.ds(s * CHANNELS + channel, TILES, stride=SIDES * CHANNELS), :] = sides[s]


def put_given(edge_ref, give_ref):
    first, last = edge_ref[pl.ds(0, TILE_ROWS), :], edge_ref[pl.ds(ROWS - TILE_ROWS, TILE_ROWS), :]
    start = lax.axis_index("tiles") % 2 == 0
    give_ref[pl.ds(0, TILE_ROWS), :] = jnp.where(start, first, last)
    give_ref[pl.ds(TILE_ROWS, TILE_ROWS), :] = jnp.where(start, last, first)


def channel_rows(ref, channel):
    return ref[pl.ds(channel, SPOTS, stride=CHANNELS), :]


def halo_places(table_ref, out_ref):
    me = lax.axis_index("tiles")
    chip, core = me // 2, me % 2
    even = chip % 2 == 0
    places = []
    for t in range(TILES):
        for s in range(SIDES):
            code = table_ref[t, s]
            tile, link = code >> 3, code & 7
            device, inner = tile // TILES, tile % TILES
            step = device // 2 - chip
            start = jnp.where((step == 1) == even, EVEN, ODD)
            own = jnp.where(device == me, OWN + inner * TILE_ROWS, OTHER)
            beside = start + jnp.where(device % 2 == core, inner * TILE_ROWS, ROWS)
            row = jnp.where(step == 0, own, beside) + (link // 2) * CHANNELS
            places.append(jnp.where(code < 0, CLOSED, row + (link % 2) * TURNED))
    _, low = position()
    channel = lax.broadcasted_iota(I32, (8, LANES), 0) % CHANNELS
    for k in range(0, SPOTS, 2):
        out_ref[pl.ds(k * CHANNELS, 8), :] = jnp.where(low, places[k], places[k + 1]) + channel


def halos(place_ref, all_ref, out_ref):
    lane, _ = position()
    back = jnp.clip(TILE - 1 - lane, 0, LANES - 1)
    for t in range(TILES):
        starts = [start + t * TILE_ROWS for start in (ODD, EVEN)]
        starts += [OWN + k * TILE_ROWS for k in (t - 1, t + 1) if 0 <= k < TILES]
        if t in (0, TILES - 1):
            starts += [OTHER, ODD + ROWS, EVEN + ROWS]
        chunks = [start // 8 + k for start in starts for k in range(TILE_ROWS // 8)]
        for h in range(TILE_ROWS // 8):
            at = pl.ds(t * TILE_ROWS + h * 8, 8)
            place = place_ref[at, :]
            chunk, row = (place & (TURNED - 1)) >> 3, place & 7
            found = jnp.zeros((8, LANES), F32)
            for k in chunks:
                picked = jnp.take_along_axis(all_ref[pl.ds(k * 8, 8), :], row, axis=0, mode="promise_in_bounds")
                found = jnp.where(chunk == k, picked, found)
            found = jnp.where((place >> 16) == 1, lane_gather(found, back), found)
            out_ref[at, :] = jnp.where(lane < TILE, found, 0.0)


def change_planes(own_a, own_b, got_a, got_b, tracers, scratch, lane, low):
    mix_a = channel_rows(own_a, tracers) * channel_rows(got_a, tracers)
    mix_b = channel_rows(own_b, tracers) * channel_rows(got_b, tracers)
    for c in range(tracers):
        own = channel_rows(own_a, c)
        scratch[pl.ds(c * SPOTS, SPOTS), :] = (
            own + mix_a * (channel_rows(got_a, c) - own) + mix_b * (channel_rows(got_b, c) - own)
        )
    out = []
    for c in range(tracers):
        sides = [scratch[pl.ds(c * SPOTS + s, TILES, stride=SIDES), :] for s in range(SIDES)]
        sides = [jnp.concatenate([side, side], axis=0) for side in sides]
        west = jnp.where(low, pltpu.roll(sides[2], 63, 1), pltpu.roll(sides[2], 63 - FIRST_HIGH, 1))
        east = jnp.where(low, sides[3], pltpu.roll(sides[3], LANES - FIRST_HIGH, 1))
        out.append([sides[0], sides[1], jnp.where(lane < 63, east, west)])
    return out


def add_columns(planes, v, lane, low):
    x, y = cell_at(lane, low, v)
    west, east = x == 0, x == TILE - 1
    index = (y + jnp.where(west, 63, 0) - jnp.where(low, 0, FIRST_HIGH)) & (LANES - 1)
    edge = west | east
    return [jnp.where(edge, lane_gather(sides[2], index), 0.0) for sides in planes]


def add_rows(ref, planes, lane, low):
    place = (CELLS - TILE - HALF) % LANES
    for c, sides in enumerate(planes):
        ref[c, 0] = ref[c, 0] + jnp.where(low, sides[0], 0.0)
        turned = pltpu.roll(sides[1], place, 1)
        ref[c, COLS - 2] = ref[c, COLS - 2] + jnp.where(low | (lane < place), 0.0, turned)
        ref[c, COLS - 1] = ref[c, COLS - 1] + jnp.where(low | (lane >= place + TILE - LANES), 0.0, turned)


def write_to(ref, *lead):
    def write(v, row, part):
        ref[(*lead, v, pl.ds(row, TILES), slice(None))] = part

    return write


def open_kernel(
    adjoint_hbm, weights_hbm, mask_hbm, near_hbm, link_hbm,
    edge_ref, give_ref, lam_ref, wet_ref, mixing_ref, spread, table_ref,
    adjoint_ref, weights_ref, mask_ref, near_ref, link_ref, sems,
):
    tracers = lam_ref.shape[0]
    pairs = (
        (mask_hbm, mask_ref),
        (weights_hbm, weights_ref),
        (adjoint_hbm, adjoint_ref),
        (near_hbm, near_ref),
        (link_hbm, link_ref),
    )
    copies = [pltpu.make_async_copy(source, target, sems.at[i]) for i, (source, target) in enumerate(pairs)]
    for copy in copies:
        copy.start()
    lane, low = position()
    copies[0].wait()
    fold(lambda a, n: mask_ref[0, :, a : a + n].astype(F32), write_to(wet_ref))
    copies[1].wait()
    fold(lambda a, n: weights_ref[0, :, a : a + n], write_to(mixing_ref))
    copies[2].wait()
    for c in range(tracers):
        fold(lambda a, n, c=c: adjoint_ref[0, c, :, a : a + n], write_to(lam_ref, c))

    def start(v, carry):
        wet = wet_ref[v]
        mixing = wet * mixing_ref[v]
        mixing_ref[v] = mixing
        for c in range(tracers):
            spread[c, v + 1] = mixing * lam_ref[c, v]
        spread[tracers, v + 1] = wet
        return carry

    loop(start)
    for c in range(tracers + 1):
        set_guards(spread, c, low)
    for p, sides in enumerate(edge_sides(lambda p, v: spread[p, v + 1], tracers + 1, lane, low)):
        put_sides(edge_ref, p, sides)
    put_given(edge_ref, give_ref)
    copies[3].wait()
    copies[4].wait()
    table_ref[...] = near_ref[...] * 8 + link_ref[...]


def inner_first_kernel(spread, lam_ref, wet_ref, mixing_ref, vertical_ref, rate_ref, pack_a, pack_b, stay_ref, keep_ref):
    tracers = lam_ref.shape[0]
    even = lax.axis_index("slab") % 2 == 0
    lane, low = position()
    fold(lambda a, n: vertical_ref[0, :, a : a + n], write_to(stay_ref))
    for c in range(tracers):
        fold(lambda a, n, c=c: 1.0 - rate_ref[c, :, a : a + n], write_to(keep_ref, c))

    def body(v, carry):
        x, _ = cell_at(lane, low, v)
        west, east = x == 0, x == TILE - 1
        wet, vertical = wet_ref[v], stay_ref[v]
        pack_a[tracers, v] = wet * jnp.where(even, 1.0, vertical)
        pack_b[tracers, v] = wet * jnp.where(even, vertical, 1.0)
        stay = 1.0 - mixing_ref[v] * inner_sum(spread, tracers, v, lane, west, east)
        stay_ref[v] = stay
        for c in range(tracers):
            moved = inner_sum(spread, c, v, lane, west, east)
            taken = (lam_ref[c, v] * stay + wet * moved) * keep_ref[c, v]
            pack_a[c, v] = taken
            pack_b[c, v] = taken
        return carry

    loop(body)


def inner_kernel(spread, lam_ref, wet_ref, stay_ref, keep_ref, out_ref):
    tracers = lam_ref.shape[0]
    lane, low = position()

    def body(v, carry):
        x, _ = cell_at(lane, low, v)
        west, east = x == 0, x == TILE - 1
        wet, stay = wet_ref[v], stay_ref[v]
        for c in range(tracers):
            moved = inner_sum(spread, c, v, lane, west, east)
            out_ref[c, v] = (lam_ref[c, v] * stay + wet * moved) * keep_ref[c, v]
        return carry

    loop(body)


def fixed_kernel(table_ref, keep_ref, pack_a, pack_b, out_a, out_b, place_ref):
    tracers = keep_ref.shape[0]
    lane, low = position()
    halo_places(table_ref, place_ref)

    def load(p, v):
        return keep_ref[p, v] if p < tracers else (pack_a if p == tracers else pack_b)[tracers, v]

    found = edge_sides(load, tracers + 2, lane, low)
    for c in range(tracers):
        put_sides(out_a, c, found[c])
        put_sides(out_b, c, found[c])
    put_sides(out_a, tracers, found[tracers])
    put_sides(out_b, tracers, found[tracers + 1])


def halo_kernel(place_ref, all_ref, edge_ref, fixed_a, fixed_b, out_a, out_b, halo_ref):
    tracers = CHANNELS - 1
    halos(place_ref, all_ref, halo_ref)
    wet, halo_wet = channel_rows(edge_ref, tracers), channel_rows(halo_ref, tracers)
    for c in range(tracers):
        change = channel_rows(fixed_a, c) * (wet * channel_rows(halo_ref, c) - channel_rows(edge_ref, c) * halo_wet)
        for out in (out_a, out_b):
            out[pl.ds(c, SPOTS, stride=CHANNELS), :] = change
    out_a[pl.ds(tracers, SPOTS, stride=CHANNELS), :] = channel_rows(fixed_a, tracers)
    out_b[pl.ds(tracers, SPOTS, stride=CHANNELS), :] = channel_rows(fixed_b, tracers)


def mix_first_kernel(pack_a, pack_b, from_b, from_a, lam_ref, mix_a_ref, mix_b_ref):
    tracers = lam_ref.shape[0]

    def body(v, carry):
        first, second = pack_a[tracers, v] * from_a[tracers, v], pack_b[tracers, v] * from_b[tracers, v]
        mix_a_ref[v] = first
        mix_b_ref[v] = second
        for c in range(tracers):
            taken = pack_a[c, v]
            lam_ref[c, v] = taken + first * (from_a[c, v] - taken) + second * (from_b[c, v] - taken)
        return carry

    loop(body)


def mix_kernel(taken_ref, from_a, from_b, mix_a_ref, mix_b_ref, wet_ref, state_ref, lam_ref, term_ref):
    tracers = lam_ref.shape[0]
    for c in range(tracers):
        fold(lambda a, n, c=c: state_ref[0, c, :, a : a + n], write_to(term_ref, c))

    def body(v, carry):
        first, second, wet = mix_a_ref[v], mix_b_ref[v], wet_ref[v]
        for c in range(tracers):
            taken = taken_ref[c, v]
            lam_ref[c, v] = taken + first * (from_a[c, v] - taken) + second * (from_b[c, v] - taken)
            term_ref[c, v] = wet * term_ref[c, v]
        return carry

    loop(body)


def middle_kernel(
    change_a, change_b, got_a, got_b, before_ref, mixing_ref, wet_edge_ref, edge_ref, give_ref, lam_ref, spread, scratch
):
    tracers = lam_ref.shape[0]
    lane, low = position()
    planes = change_planes(change_a, change_b, got_a, got_b, tracers, scratch, lane, low)

    def body(v, carry):
        extra = add_columns(planes, v, lane, low)
        mixing = mixing_ref[v]
        for c in range(tracers):
            lam = before_ref[c, v] + extra[c]
            lam_ref[c, v] = lam
            spread[c, v + 1] = mixing * lam
        return carry

    loop(body)
    add_rows(lam_ref, planes, lane, low)
    for c in range(tracers):
        for v in (0, COLS - 2, COLS - 1):
            spread[c, v + 1] = mixing_ref[v] * lam_ref[c, v]
        set_guards(spread, c, low)
    for p, sides in enumerate(edge_sides(lambda p, v: spread[p, v + 1], tracers, lane, low)):
        put_sides(edge_ref, p, sides)
    edge_ref[pl.ds(tracers, SPOTS, stride=CHANNELS), :] = channel_rows(wet_edge_ref, tracers)
    put_given(edge_ref, give_ref)


def close_kernel(
    owner_hbm, change_a, change_b, got_a, got_b, before_ref, weighted_ref,
    out_hbm, part_ref, lam_ref, term_ref, rows_ref, sums_ref, flat_ref, scratch, owner_ref, sems,
):
    tracers = lam_ref.shape[0]
    owner_copy = pltpu.make_async_copy(owner_hbm, owner_ref, sems.at[tracers])
    owner_copy.start()
    lane, low = position()
    planes = change_planes(change_a, change_b, got_a, got_b, tracers, scratch, lane, low)

    def body(v, carry):
        extra = add_columns(planes, v, lane, low)
        for c in range(tracers):
            lam = before_ref[c, v] + extra[c]
            lam_ref[c, v] = lam
            term_ref[c, v] = weighted_ref[c, v] * lam
        return carry

    loop(body)
    add_rows(lam_ref, planes, lane, low)
    for c in range(tracers):
        for v in (0, COLS - 2, COLS - 1):
            term_ref[c, v] = weighted_ref[c, v] * lam_ref[c, v]
    copies = []
    for c in range(tracers):
        for v in range(COLS):
            values = lam_ref[c, v]
            flat_ref[0, c, :, v * LANES : (v + 1) * LANES] = values[:TILES]
            start = HALF + v * LANES
            width = min(LANES, CELLS - start)
            flat_ref[0, c, :, start : start + width] = values[TILES:, :width]
        copies.append(pltpu.make_async_copy(flat_ref.at[0, c], out_hbm.at[0, c], sems.at[c]))
        copies[-1].start()
    for c in range(tracers):
        guard = pltpu.roll(term_ref[c, 0], TILES, 0)
        for block in range(COARSE):
            total = [None, None]
            for y in range(block * BLOCK, (block + 1) * BLOCK):
                half = y * TILE // HALF
                v, shift = divmod(y * TILE - half * HALF, LANES)
                values = term_ref[c, v]
                if shift + TILE > LANES:
                    after = term_ref[c, v + 1] if v + 1 < COLS else guard
                    values = jnp.where(lane >= shift, values, after)
                if shift:
                    values = pltpu.roll(values, LANES - shift, 1)
                total[half] = values if total[half] is None else total[half] + values
            parts = [total[h][h * TILES : (h + 1) * TILES] for h in range(2) if total[h] is not None]
            summed = parts[0] if len(parts) == 1 else parts[0] + parts[1]
            summed = jnp.where(lane[:TILES] < TILE, summed, 0.0)
            rows_ref[pl.ds((c * COARSE + block) * TILES, TILES), :] = summed
    lane_in = lax.broadcasted_iota(I32, (LANES, LANES), 0)
    lane_out = lax.broadcasted_iota(I32, (LANES, LANES), 1)
    low_edge = lane_out * BLOCK
    pick = ((lane_in >= low_edge) & (lane_in < low_edge + BLOCK) & (lane_out < COARSE)).astype(jnp.bfloat16)
    left = rows_ref[...]
    summed = jnp.zeros_like(left)
    for _ in range(3):
        part = left.astype(jnp.bfloat16)
        summed = summed + jnp.dot(part, pick, preferred_element_type=F32)
        left = left - part.astype(F32)
    sums_ref[...] = summed
    for spot in range(8):
        total = jnp.zeros((TILES, LANES), F32)
        for k in range(tracers * COARSE):
            start = k * COARSE - spot * LANES
            if start >= LANES or start + COARSE <= 0:
                continue
            values = sums_ref[pl.ds(k * TILES, TILES), :]
            values = pltpu.roll(values, start % LANES, 1) if start % LANES else values
            if start < 0:
                values = jnp.where(lane[:TILES] < start + COARSE, values, 0.0)
            elif start + COARSE > LANES:
                values = jnp.where(lane[:TILES] >= start, values, 0.0)
            total = total + values
        rows_ref[pl.ds(spot, TILES, stride=8), :] = total
    part_ref[...] = jnp.zeros_like(part_ref)
    me = lax.axis_index("tiles")
    owner_copy.wait()
    for t in range(TILES):
        owner = owner_ref[me * TILES + t]
        part_ref[owner] = part_ref[owner] + rows_ref[pl.ds(t * 8, 8), :]
    for copy in copies:
        copy.wait()


def swaps(count, width=1):
    found = []
    for first in (0, 1):
        found.append(
            [
                pair
                for i in range(first, count // width - 1, 2)
                for k in range(width)
                for pair in ((i * width + k, (i + 1) * width + k), ((i + 1) * width + k, i * width + k))
            ]
        )
    return found


VMEM, SMEM, HBM = (pl.BlockSpec(memory_space=space) for space in (pltpu.VMEM, pltpu.SMEM, pltpu.HBM))


def call(kernel, ins, out, scratch, outs=None):
    return pl.pallas_call(
        kernel,
        out_shape=[jax.ShapeDtypeStruct(shape, F32) if isinstance(shape, tuple) else shape for shape in out],
        in_specs=ins,
        out_specs=outs or [VMEM] * len(out),
        scratch_shapes=[pltpu.VMEM(shape, F32) if isinstance(shape, tuple) else shape for shape in scratch],
        compiler_params=pltpu.CompilerParams(vmem_limit_bytes=32 * 1024 * 1024),
        name=kernel.__name__,
    )


def shards(adjoint, state, weights, vertical, mask, rate, neighbours, links, owners):
    tracers = adjoint.shape[1]
    number = lax.axis_size("tiles")
    even_swap, odd_swap = swaps(lax.axis_size("slab"))
    core_swap = [(2 * i + a, 2 * i + 1 - a) for i in range(number // 2) for a in range(2)]
    even_chips, odd_chips = swaps(number, 2)
    passing = swaps(number, 4)[0]
    plane = (COLS, 8, LANES)
    planes = (tracers, *plane)
    pack = (tracers + 1, *plane)
    guarded = (COLS + 2, 8, LANES)
    edges = (ROWS, LANES)
    given = (2 * TILE_ROWS, LANES)

    def around(edge, other):
        shown = jnp.concatenate([edge, other[:TILE_ROWS]])
        even = lax.ppermute(shown, "tiles", even_chips)
        if number == 8:
            odd = lax.ppermute(even, "tiles", passing)
        else:
            odd = lax.ppermute(shown, "tiles", odd_chips)
        return jnp.concatenate([even, shown, odd, other[TILE_ROWS:]])

    def across(first, second):
        return lax.ppermute(first, "slab", even_swap), lax.ppermute(second, "slab", odd_swap)

    edge, give, lam, wet, mixing, spread, table = call(
        open_kernel,
        [HBM] * 5,
        [edges, given, planes, plane, plane, (tracers + 1, *guarded), jax.ShapeDtypeStruct(links.shape, I32)],
        [adjoint.shape, weights.shape]
        + [pltpu.VMEM(table.shape, I32) for table in (mask, neighbours, links)]
        + [pltpu.SemaphoreType.DMA((5,))],
    )(*(pltpu.with_memory_space_constraint(x, pltpu.HBM) for x in (adjoint, weights, mask, neighbours, links)))
    other = lax.ppermute(give, "tiles", core_swap)
    pack_a, pack_b, stay, keep = call(inner_first_kernel, [VMEM] * 6, [pack, pack, plane, planes], [])(
        spread, lam, wet, mixing, vertical, rate
    )
    pack_a, pack_b, other = lax.optimization_barrier((pack_a, pack_b, other))
    from_a, from_b = across(pack_a, pack_b)
    near = around(edge, other)
    fixed_a, fixed_b, places = call(
        fixed_kernel, [SMEM] + [VMEM] * 3, [edges] * 2 + [jax.ShapeDtypeStruct(edges, I32)], []
    )(table, keep, pack_a, pack_b)
    halo = call(halo_kernel, [VMEM] * 5, [edges] * 2, [edges])
    change_a, change_b = halo(places, near, edge, fixed_a, fixed_b)
    got_a, got_b = across(change_a, change_b)
    before, mix_a, mix_b = call(mix_first_kernel, [VMEM] * 4, [planes, plane, plane], [])(
        pack_a, pack_b, from_b, from_a
    )
    edge, give, lam, spread = call(middle_kernel, [VMEM] * 7, [edges, given, planes, (tracers, *guarded)], [edges])(
        change_a, change_b, got_a, got_b, before, mixing, edge
    )
    other = lax.ppermute(give, "tiles", core_swap)
    (taken,) = call(inner_kernel, [VMEM] * 5, [planes], [])(spread, lam, wet, stay, keep)
    taken, other = lax.optimization_barrier((taken, other))
    from_a, from_b = across(taken, taken)
    near = around(edge, other)
    change_a, change_b = halo(places, near, edge, fixed_a, fixed_b)
    got_a, got_b = across(change_a, change_b)
    before, weighted = call(mix_kernel, [VMEM] * 7, [planes, planes], [])(
        taken, from_a, from_b, mix_a, mix_b, wet, state
    )
    sums = (tracers * COARSE * TILES + 4, LANES)
    out, part = call(
        close_kernel,
        [HBM] + [VMEM] * 6,
        [adjoint.shape, (number, 8, LANES)],
        [planes, planes, sums, sums, adjoint.shape, edges]
        + [pltpu.SMEM(owners.shape, I32), pltpu.SemaphoreType.DMA((tracers + 1,))],
        [HBM, VMEM],
    )(pltpu.with_memory_space_constraint(owners, pltpu.HBM), change_a, change_b, got_a, got_b, before, weighted)
    part = lax.all_to_all(part, "tiles", 0, 0, tiled=True)
    gradient = part.sum(axis=0).reshape(1, 1, 8 * LANES)[:, :, : tracers * COARSE * COARSE]
    return out, gradient


def solution(mesh):
    placed = (
        P("slab", None, "tiles", None),
        P("slab", None, "tiles", None),
        P("slab", "tiles", None),
        P("slab", "tiles", None),
        P("slab", "tiles", None),
        P(None, "tiles", None),
        P("tiles", None),
        P("tiles", None),
        P(),
    )
    return jax.shard_map(
        shards,
        mesh=mesh,
        in_specs=placed,
        out_specs=(P("slab", None, "tiles", None), P("slab", "tiles", None)),
        check_vma=False,
    )
```

```python
import functools

import jax
import jax.numpy as jnp
from jax import lax
from jax.experimental import pallas as pl
from jax.experimental.pallas import tpu as pltpu
from jax.sharding import PartitionSpec as P

TILE = 90
CELLS = TILE * TILE
SUBSTEPS = 2
BLOCK = 6
COARSE = 15
LANES = 128
COLS = 32
HALF = COLS * LANES
TILES = 4
SIDES = 4
SPOTS = TILES * SIDES
CHANNELS = 4
ROWS = SPOTS * CHANNELS
TILE_ROWS = SIDES * CHANNELS
SHOWN = ROWS + TILE_ROWS
FIRST = {"odd": 0, "even": SHOWN, "shown": SHOWN + SHOWN, "other": SHOWN + SHOWN + SHOWN}
SECOND = {"even": 0, "shown": SHOWN, "odd": SHOWN + SHOWN, "other": SHOWN + SHOWN + SHOWN}
CLOSED = -8
TURNED = 1 << 16
FIRST_HIGH = HALF // TILE
UNROLL = 32
F32 = jnp.float32
I32 = jnp.int32


def position():
    lane = lax.broadcasted_iota(I32, (8, LANES), 1)
    low = lax.broadcasted_iota(I32, (8, LANES), 0) < TILES
    return lane, low


def cell_at(lane, low, v):
    cell = lane + jnp.where(low, 0, HALF) + v * LANES
    y = (cell * 46604) >> 22
    return cell - y * TILE, y


def lane_gather(values, index):
    return jnp.take_along_axis(values, index, axis=1, mode="promise_in_bounds")


def loop(body, carry=0):
    return lax.fori_loop(0, COLS, body, carry, unroll=UNROLL)


def fold(read, write):
    for v in range(COLS):
        write(v, 0, read(v * LANES, LANES))
        start = HALF + v * LANES
        width = min(LANES, CELLS - start)
        part = read(start, width)
        if width < LANES:
            part = jnp.concatenate([part, jnp.zeros((TILES, LANES - width), F32)], axis=1)
        write(v, TILES, part)


def set_guards(ref, plane, low):
    first, last = ref[plane, 1], ref[plane, COLS]
    ref[plane, 0] = jnp.where(low, 0.0, pltpu.roll(last, TILES, 0))
    ref[plane, COLS + 1] = jnp.where(low, pltpu.roll(first, TILES, 0), 0.0)


def inner_sum(ref, plane, v, lane, west, east):
    before, here, after = ref[plane, v], ref[plane, v + 1], ref[plane, v + 2]
    left = pltpu.roll(jnp.where(lane < LANES - 1, here, before), 1, 1)
    right = pltpu.roll(jnp.where(lane >= 1, here, after), LANES - 1, 1)
    up = pltpu.roll(jnp.where(lane < LANES - TILE, here, before), TILE, 1)
    down = pltpu.roll(jnp.where(lane >= TILE, here, after), LANES - TILE, 1)
    return jnp.where(west, 0.0, left) + jnp.where(east, 0.0, right) + (up + down)


def edge_sides(load, planes, lane, low):
    step = lane & 63
    base = TILE * step + jnp.where(low, 0, FIRST_HIGH * TILE - HALF) + jnp.where(lane < 64, TILE - 1, TILE)
    index, column = base & (LANES - 1), base >> 7

    def body(v, found):
        hit = column == v
        return tuple(jnp.where(hit, lane_gather(load(p, v), index), found[p]) for p in range(planes))

    found = loop(body, tuple(jnp.zeros((8, LANES), F32) for _ in range(planes)))
    bottom = CELLS - TILE - HALF + lane
    edge = lane < TILE
    first_low = jnp.where(low, lane + 63, lane - FIRST_HIGH + 63) & (LANES - 1)
    last_low = jnp.where(low, lane, lane - FIRST_HIGH) & (LANES - 1)
    out = []
    for p in range(planes):
        top = load(p, 0)
        picked = jnp.where(
            (bottom >> 7) == COLS - 2,
            lane_gather(load(p, COLS - 2), bottom & (LANES - 1)),
            lane_gather(load(p, COLS - 1), bottom & (LANES - 1)),
        )
        west, east = lane_gather(found[p], first_low), lane_gather(found[p], last_low)
        west = jnp.where(low, jnp.where(lane == 0, top, west), west)
        west_low, east_low = west[:TILES], east[:TILES]
        here = lane[:TILES]
        west = jnp.where(here <= FIRST_HIGH, west_low, west[TILES:])
        east = jnp.where(here < FIRST_HIGH, east_low, east[TILES:])
        inside = here < TILE
        out.append(
            [
                jnp.where(inside, top[:TILES], 0.0),
                jnp.where(inside, picked[TILES:], 0.0),
                jnp.where(inside, west, 0.0),
                jnp.where(inside, east, 0.0),
            ]
        )
    return out


def put_sides(ref, channel, sides):
    for s in range(SIDES):
        ref[pl.ds(s * CHANNELS + channel, TILES, stride=SIDES * CHANNELS), :] = sides[s]


def put_given(edge_ref, give_ref):
    first, last = edge_ref[pl.ds(0, TILE_ROWS), :], edge_ref[pl.ds(ROWS - TILE_ROWS, TILE_ROWS), :]
    start = lax.axis_index("tiles") % 2 == 0
    give_ref[pl.ds(0, TILE_ROWS), :] = jnp.where(start, first, last)
    give_ref[pl.ds(TILE_ROWS, TILE_ROWS), :] = jnp.where(start, last, first)


def channel_rows(ref, channel):
    return ref[pl.ds(channel, SPOTS, stride=CHANNELS), :]


def halo_places(table_ref, out_ref, layout):
    me = lax.axis_index("tiles")
    chip, core = me // 2, me % 2
    even = chip % 2 == 0
    places = []
    for t in range(TILES):
        for s in range(SIDES):
            code = table_ref[t, s]
            tile, link = code >> 3, code & 7
            device, inner = tile // TILES, tile % TILES
            step = device // 2 - chip
            start = jnp.where((step == 1) == even, layout["even"], layout["odd"])
            own = jnp.where(device == me, layout["shown"] + inner * TILE_ROWS, layout["other"])
            beside = start + jnp.where(device % 2 == core, inner * TILE_ROWS, ROWS)
            row = jnp.where(step == 0, own, beside) + (link // 2) * CHANNELS
            places.append(jnp.where(code < 0, CLOSED, row + (link % 2) * TURNED))
    _, low = position()
    channel = lax.broadcasted_iota(I32, (8, LANES), 0) % CHANNELS
    for k in range(0, SPOTS, 2):
        out_ref[pl.ds(k * CHANNELS, 8), :] = jnp.where(low, places[k], places[k + 1]) + channel


def halos(place_ref, all_ref, out_ref, layout):
    lane, _ = position()
    back = jnp.clip(TILE - 1 - lane, 0, LANES - 1)
    for t in range(TILES):
        starts = [start + t * TILE_ROWS for start in (layout["odd"], layout["even"])]
        starts += [layout["shown"] + k * TILE_ROWS for k in (t - 1, t + 1) if 0 <= k < TILES]
        if t in (0, TILES - 1):
            starts += [layout["other"], layout["odd"] + ROWS, layout["even"] + ROWS]
        chunks = [start // 8 + k for start in starts for k in range(TILE_ROWS // 8)]
        for h in range(TILE_ROWS // 8):
            at = pl.ds(t * TILE_ROWS + h * 8, 8)
            place = place_ref[at, :]
            chunk, row = (place & (TURNED - 1)) >> 3, place & 7
            found = jnp.zeros((8, LANES), F32)
            for k in chunks:
                picked = jnp.take_along_axis(all_ref[pl.ds(k * 8, 8), :], row, axis=0, mode="promise_in_bounds")
                found = jnp.where(chunk == k, picked, found)
            found = jnp.where((place >> 16) == 1, lane_gather(found, back), found)
            out_ref[at, :] = jnp.where(lane < TILE, found, 0.0)


def change_planes(own_a, own_b, got_a, got_b, tracers, scratch, lane, low):
    mix_a = channel_rows(own_a, tracers) * channel_rows(got_a, tracers)
    mix_b = channel_rows(own_b, tracers) * channel_rows(got_b, tracers)
    for c in range(tracers):
        own = channel_rows(own_a, c)
        scratch[pl.ds(c * SPOTS, SPOTS), :] = (
            own + mix_a * (channel_rows(got_a, c) - own) + mix_b * (channel_rows(got_b, c) - own)
        )
    out = []
    for c in range(tracers):
        sides = [scratch[pl.ds(c * SPOTS + s, TILES, stride=SIDES), :] for s in range(SIDES)]
        sides = [jnp.concatenate([side, side], axis=0) for side in sides]
        west = jnp.where(low, pltpu.roll(sides[2], 63, 1), pltpu.roll(sides[2], 63 - FIRST_HIGH, 1))
        east = jnp.where(low, sides[3], pltpu.roll(sides[3], LANES - FIRST_HIGH, 1))
        out.append([sides[0], sides[1], jnp.where(lane < 63, east, west)])
    return out


def add_columns(planes, v, lane, low):
    x, y = cell_at(lane, low, v)
    west, east = x == 0, x == TILE - 1
    index = (y + jnp.where(west, 63, 0) - jnp.where(low, 0, FIRST_HIGH)) & (LANES - 1)
    edge = west | east
    return [jnp.where(edge, lane_gather(sides[2], index), 0.0) for sides in planes]


def add_rows(ref, planes, lane, low):
    place = (CELLS - TILE - HALF) % LANES
    for c, sides in enumerate(planes):
        ref[c, 0] = ref[c, 0] + jnp.where(low, sides[0], 0.0)
        turned = pltpu.roll(sides[1], place, 1)
        ref[c, COLS - 2] = ref[c, COLS - 2] + jnp.where(low | (lane < place), 0.0, turned)
        ref[c, COLS - 1] = ref[c, COLS - 1] + jnp.where(low | (lane >= place + TILE - LANES), 0.0, turned)


def write_to(ref, *lead):
    def write(v, row, part):
        ref[(*lead, v, pl.ds(row, TILES), slice(None))] = part

    return write


def open_kernel(
    adjoint_hbm, weights_hbm, mask_hbm, near_hbm, link_hbm,
    edge_ref, give_ref, lam_ref, wet_ref, mixing_ref, spread, table_ref,
    adjoint_ref, weights_ref, mask_ref, near_ref, link_ref, sems,
):
    tracers = lam_ref.shape[0]
    pairs = (
        (mask_hbm, mask_ref),
        (weights_hbm, weights_ref),
        (adjoint_hbm, adjoint_ref),
        (near_hbm, near_ref),
        (link_hbm, link_ref),
    )
    copies = [pltpu.make_async_copy(source, target, sems.at[i]) for i, (source, target) in enumerate(pairs)]
    for copy in copies:
        copy.start()
    lane, low = position()
    copies[0].wait()
    fold(lambda a, n: mask_ref[0, :, a : a + n].astype(F32), write_to(wet_ref))
    copies[1].wait()
    fold(lambda a, n: weights_ref[0, :, a : a + n], write_to(mixing_ref))
    copies[2].wait()
    for c in range(tracers):
        fold(lambda a, n, c=c: adjoint_ref[0, c, :, a : a + n], write_to(lam_ref, c))

    def start(v, carry):
        wet = wet_ref[v]
        mixing = wet * mixing_ref[v]
        mixing_ref[v] = mixing
        for c in range(tracers):
            spread[c, v + 1] = mixing * lam_ref[c, v]
        spread[tracers, v + 1] = wet
        return carry

    loop(start)
    for c in range(tracers + 1):
        set_guards(spread, c, low)
    for p, sides in enumerate(edge_sides(lambda p, v: spread[p, v + 1], tracers + 1, lane, low)):
        put_sides(edge_ref, p, sides)
    put_given(edge_ref, give_ref)
    copies[3].wait()
    copies[4].wait()
    table_ref[...] = near_ref[...] * 8 + link_ref[...]


def inner_first_kernel(spread, lam_ref, wet_ref, mixing_ref, vertical_ref, rate_ref, pack_a, pack_b, stay_ref, keep_ref):
    tracers = lam_ref.shape[0]
    level, levels = lax.axis_index("slab"), lax.axis_size("slab")
    even = level % 2 == 0
    has_a = (level // 2 * 2 + 1 < levels).astype(F32)
    has_b = ((level >= 1) & ((level + 1) // 2 * 2 < levels)).astype(F32)
    for_a = has_a * jnp.where(even, 1.0, 0.0), has_a * jnp.where(even, 0.0, 1.0)
    for_b = has_b * jnp.where(even, 0.0, 1.0), has_b * jnp.where(even, 1.0, 0.0)
    lane, low = position()
    fold(lambda a, n: vertical_ref[0, :, a : a + n], write_to(stay_ref))
    for c in range(tracers):
        fold(lambda a, n, c=c: 1.0 - rate_ref[c, :, a : a + n], write_to(keep_ref, c))

    def body(v, carry):
        x, _ = cell_at(lane, low, v)
        west, east = x == 0, x == TILE - 1
        wet, vertical = wet_ref[v], stay_ref[v]
        pack_a[tracers, v] = wet * (for_a[0] + for_a[1] * vertical)
        pack_b[tracers, v] = wet * (for_b[0] + for_b[1] * vertical)
        stay = 1.0 - mixing_ref[v] * inner_sum(spread, tracers, v, lane, west, east)
        stay_ref[v] = stay
        for c in range(tracers):
            moved = inner_sum(spread, c, v, lane, west, east)
            taken = (lam_ref[c, v] * stay + wet * moved) * keep_ref[c, v]
            pack_a[c, v] = taken
            pack_b[c, v] = taken
        return carry

    loop(body)


def inner_kernel(spread, lam_ref, wet_ref, stay_ref, keep_ref, out_ref):
    tracers = lam_ref.shape[0]
    lane, low = position()

    def body(v, carry):
        x, _ = cell_at(lane, low, v)
        west, east = x == 0, x == TILE - 1
        wet, stay = wet_ref[v], stay_ref[v]
        for c in range(tracers):
            moved = inner_sum(spread, c, v, lane, west, east)
            out_ref[c, v] = (lam_ref[c, v] * stay + wet * moved) * keep_ref[c, v]
        return carry

    loop(body)


def fixed_kernel(table_ref, keep_ref, pack_a, pack_b, out_a, out_b, first_ref, second_ref):
    tracers = keep_ref.shape[0]
    lane, low = position()
    halo_places(table_ref, first_ref, FIRST)
    halo_places(table_ref, second_ref, SECOND)

    def load(p, v):
        return keep_ref[p, v] if p < tracers else (pack_a if p == tracers else pack_b)[tracers, v]

    found = edge_sides(load, tracers + 2, lane, low)
    for c in range(tracers):
        put_sides(out_a, c, found[c])
        put_sides(out_b, c, found[c])
    put_sides(out_a, tracers, found[tracers])
    put_sides(out_b, tracers, found[tracers + 1])


def halo_kernel(layout, place_ref, all_ref, edge_ref, fixed_a, fixed_b, out_a, out_b, halo_ref):
    tracers = CHANNELS - 1
    halos(place_ref, all_ref, halo_ref, layout)
    wet, halo_wet = channel_rows(edge_ref, tracers), channel_rows(halo_ref, tracers)
    for c in range(tracers):
        change = channel_rows(fixed_a, c) * (wet * channel_rows(halo_ref, c) - channel_rows(edge_ref, c) * halo_wet)
        for out in (out_a, out_b):
            out[pl.ds(c, SPOTS, stride=CHANNELS), :] = change
    out_a[pl.ds(tracers, SPOTS, stride=CHANNELS), :] = channel_rows(fixed_a, tracers)
    out_b[pl.ds(tracers, SPOTS, stride=CHANNELS), :] = channel_rows(fixed_b, tracers)


def mix_first_kernel(pack_a, pack_b, from_b, from_a, lam_ref, mix_a_ref, mix_b_ref):
    tracers = lam_ref.shape[0]

    def body(v, carry):
        first, second = pack_a[tracers, v] * from_a[tracers, v], pack_b[tracers, v] * from_b[tracers, v]
        mix_a_ref[v] = first
        mix_b_ref[v] = second
        for c in range(tracers):
            taken = pack_a[c, v]
            lam_ref[c, v] = taken + first * (from_a[c, v] - taken) + second * (from_b[c, v] - taken)
        return carry

    loop(body)


def mix_kernel(taken_ref, from_a, from_b, mix_a_ref, mix_b_ref, wet_ref, state_ref, lam_ref, term_ref):
    tracers = lam_ref.shape[0]
    for c in range(tracers):
        fold(lambda a, n, c=c: state_ref[0, c, :, a : a + n], write_to(term_ref, c))

    def body(v, carry):
        first, second, wet = mix_a_ref[v], mix_b_ref[v], wet_ref[v]
        for c in range(tracers):
            taken = taken_ref[c, v]
            lam_ref[c, v] = taken + first * (from_a[c, v] - taken) + second * (from_b[c, v] - taken)
            term_ref[c, v] = wet * term_ref[c, v]
        return carry

    loop(body)


def middle_kernel(
    change_a, change_b, got_a, got_b, before_ref, mixing_ref, wet_edge_ref, edge_ref, give_ref, lam_ref, spread, scratch
):
    tracers = lam_ref.shape[0]
    lane, low = position()
    planes = change_planes(change_a, change_b, got_a, got_b, tracers, scratch, lane, low)

    def body(v, carry):
        extra = add_columns(planes, v, lane, low)
        mixing = mixing_ref[v]
        for c in range(tracers):
            lam = before_ref[c, v] + extra[c]
            lam_ref[c, v] = lam
            spread[c, v + 1] = mixing * lam
        return carry

    loop(body)
    add_rows(lam_ref, planes, lane, low)
    for c in range(tracers):
        for v in (0, COLS - 2, COLS - 1):
            spread[c, v + 1] = mixing_ref[v] * lam_ref[c, v]
        set_guards(spread, c, low)
    for p, sides in enumerate(edge_sides(lambda p, v: spread[p, v + 1], tracers, lane, low)):
        put_sides(edge_ref, p, sides)
    edge_ref[pl.ds(tracers, SPOTS, stride=CHANNELS), :] = channel_rows(wet_edge_ref, tracers)
    put_given(edge_ref, give_ref)


def close_kernel(
    owner_hbm, change_a, change_b, got_a, got_b, before_ref, weighted_ref,
    out_hbm, part_ref, lam_ref, term_ref, rows_ref, sums_ref, flat_ref, scratch, owner_ref, sems,
):
    tracers = lam_ref.shape[0]
    owner_copy = pltpu.make_async_copy(owner_hbm, owner_ref, sems.at[tracers])
    owner_copy.start()
    lane, low = position()
    planes = change_planes(change_a, change_b, got_a, got_b, tracers, scratch, lane, low)

    def body(v, carry):
        extra = add_columns(planes, v, lane, low)
        for c in range(tracers):
            lam = before_ref[c, v] + extra[c]
            lam_ref[c, v] = lam
            term_ref[c, v] = weighted_ref[c, v] * lam
        return carry

    loop(body)
    add_rows(lam_ref, planes, lane, low)
    for c in range(tracers):
        for v in (0, COLS - 2, COLS - 1):
            term_ref[c, v] = weighted_ref[c, v] * lam_ref[c, v]
    copies = []
    for c in range(tracers):
        for v in range(COLS):
            values = lam_ref[c, v]
            flat_ref[0, c, :, v * LANES : (v + 1) * LANES] = values[:TILES]
            start = HALF + v * LANES
            width = min(LANES, CELLS - start)
            flat_ref[0, c, :, start : start + width] = values[TILES:, :width]
        copies.append(pltpu.make_async_copy(flat_ref.at[0, c], out_hbm.at[0, c], sems.at[c]))
        copies[-1].start()
    for c in range(tracers):
        guard = pltpu.roll(term_ref[c, 0], TILES, 0)
        for block in range(COARSE):
            total = [None, None]
            for y in range(block * BLOCK, (block + 1) * BLOCK):
                half = y * TILE // HALF
                v, shift = divmod(y * TILE - half * HALF, LANES)
                values = term_ref[c, v]
                if shift + TILE > LANES:
                    after = term_ref[c, v + 1] if v + 1 < COLS else guard
                    values = jnp.where(lane >= shift, values, after)
                if shift:
                    values = pltpu.roll(values, LANES - shift, 1)
                total[half] = values if total[half] is None else total[half] + values
            parts = [total[h][h * TILES : (h + 1) * TILES] for h in range(2) if total[h] is not None]
            summed = parts[0] if len(parts) == 1 else parts[0] + parts[1]
            summed = jnp.where(lane[:TILES] < TILE, summed, 0.0)
            rows_ref[pl.ds((c * COARSE + block) * TILES, TILES), :] = summed
    lane_in = lax.broadcasted_iota(I32, (LANES, LANES), 0)
    lane_out = lax.broadcasted_iota(I32, (LANES, LANES), 1)
    low_edge = lane_out * BLOCK
    pick = ((lane_in >= low_edge) & (lane_in < low_edge + BLOCK) & (lane_out < COARSE)).astype(jnp.bfloat16)
    left = rows_ref[...]
    summed = jnp.zeros_like(left)
    for _ in range(3):
        part = left.astype(jnp.bfloat16)
        summed = summed + jnp.dot(part, pick, preferred_element_type=F32)
        left = left - part.astype(F32)
    sums_ref[...] = summed
    for spot in range(8):
        total = jnp.zeros((TILES, LANES), F32)
        for k in range(tracers * COARSE):
            start = k * COARSE - spot * LANES
            if start >= LANES or start + COARSE <= 0:
                continue
            values = sums_ref[pl.ds(k * TILES, TILES), :]
            values = pltpu.roll(values, start % LANES, 1) if start % LANES else values
            if start < 0:
                values = jnp.where(lane[:TILES] < start + COARSE, values, 0.0)
            elif start + COARSE > LANES:
                values = jnp.where(lane[:TILES] >= start, values, 0.0)
            total = total + values
        rows_ref[pl.ds(spot, TILES, stride=8), :] = total
    part_ref[...] = jnp.zeros_like(part_ref)
    me = lax.axis_index("tiles")
    owner_copy.wait()
    for t in range(TILES):
        owner = owner_ref[me * TILES + t]
        part_ref[owner] = part_ref[owner] + rows_ref[pl.ds(t * 8, 8), :]
    for copy in copies:
        copy.wait()


def swaps(count, width=1):
    found = []
    for first in (0, 1):
        found.append(
            [
                pair
                for i in range(first, count // width - 1, 2)
                for k in range(width)
                for pair in ((i * width + k, (i + 1) * width + k), ((i + 1) * width + k, i * width + k))
            ]
        )
    return found


VMEM, SMEM, HBM = (pl.BlockSpec(memory_space=space) for space in (pltpu.VMEM, pltpu.SMEM, pltpu.HBM))


def call(kernel, ins, out, scratch, outs=None):
    return pl.pallas_call(
        kernel,
        out_shape=[jax.ShapeDtypeStruct(shape, F32) if isinstance(shape, tuple) else shape for shape in out],
        in_specs=ins,
        out_specs=outs or [VMEM] * len(out),
        scratch_shapes=[pltpu.VMEM(shape, F32) if isinstance(shape, tuple) else shape for shape in scratch],
        compiler_params=pltpu.CompilerParams(vmem_limit_bytes=32 * 1024 * 1024),
        name=getattr(kernel, "func", kernel).__name__,
    )


def shards(adjoint, state, weights, vertical, mask, rate, neighbours, links, owners):
    tracers = adjoint.shape[1]
    number = lax.axis_size("tiles")
    levels = lax.axis_size("slab")
    even_swap, odd_swap = ([(k * levels + i, k * levels + j) for i, j in pairs for k in range(number)] for pairs in swaps(levels))
    core_swap = [(2 * i + a, 2 * i + 1 - a) for i in range(number // 2) for a in range(2)]
    for pairs in (even_swap, odd_swap):
        alone = set(range(levels)) - {i % levels for i, _ in pairs}
        pairs.extend((a * levels + i, b * levels + i) for i in sorted(alone) for a, b in core_swap)
    even_chips, odd_chips = swaps(number, 2)
    passing = swaps(number, 4)[0]
    plane = (COLS, 8, LANES)
    planes = (tracers, *plane)
    pack = (tracers + 1, *plane)
    guarded = (COLS + 2, 8, LANES)
    edges = (ROWS, LANES)
    given = (2 * TILE_ROWS, LANES)

    def around(edge, other, layout):
        shown = jnp.concatenate([edge, other[:TILE_ROWS]])
        even = lax.ppermute(shown, "tiles", even_chips)
        if number == 8:
            odd = lax.ppermute(even, "tiles", passing)
        else:
            odd = lax.ppermute(shown, "tiles", odd_chips)
        parts = {"even": even, "shown": shown, "odd": odd, "other": other[TILE_ROWS:]}
        return jnp.concatenate([parts[name] for name in layout])

    def across(first, second):
        return lax.ppermute(first, ("tiles", "slab"), even_swap), lax.ppermute(second, ("tiles", "slab"), odd_swap)

    edge, give, lam, wet, mixing, spread, table = call(
        open_kernel,
        [HBM] * 5,
        [edges, given, planes, plane, plane, (tracers + 1, *guarded), jax.ShapeDtypeStruct(links.shape, I32)],
        [adjoint.shape, weights.shape]
        + [pltpu.VMEM(table.shape, I32) for table in (mask, neighbours, links)]
        + [pltpu.SemaphoreType.DMA((5,))],
    )(*(pltpu.with_memory_space_constraint(x, pltpu.HBM) for x in (adjoint, weights, mask, neighbours, links)))
    other = lax.ppermute(give, "tiles", core_swap)
    pack_a, pack_b, stay, keep = call(inner_first_kernel, [VMEM] * 6, [pack, pack, plane, planes], [])(
        spread, lam, wet, mixing, vertical, rate
    )
    pack_a, pack_b, other = lax.optimization_barrier((pack_a, pack_b, other))
    from_a, from_b = across(pack_a, pack_b)
    near = around(edge, other, FIRST)
    fixed_a, fixed_b, first, second = call(
        fixed_kernel, [SMEM] + [VMEM] * 3, [edges] * 2 + [jax.ShapeDtypeStruct(edges, I32)] * 2, []
    )(table, keep, pack_a, pack_b)

    def halo(layout, *args):
        return call(functools.partial(halo_kernel, layout), [VMEM] * 5, [edges] * 2, [edges])(*args)

    change_a, change_b = halo(FIRST, first, near, edge, fixed_a, fixed_b)
    got_a, got_b = across(change_a, change_b)
    before, mix_a, mix_b = call(mix_first_kernel, [VMEM] * 4, [planes, plane, plane], [])(
        pack_a, pack_b, from_b, from_a
    )
    edge, give, lam, spread = call(middle_kernel, [VMEM] * 7, [edges, given, planes, (tracers, *guarded)], [edges])(
        change_a, change_b, got_a, got_b, before, mixing, edge
    )
    other = lax.ppermute(give, "tiles", core_swap)
    (taken,) = call(inner_kernel, [VMEM] * 5, [planes], [])(spread, lam, wet, stay, keep)
    taken, other = lax.optimization_barrier((taken, other))
    from_a, from_b = across(taken, taken)
    near = around(edge, other, SECOND)
    change_a, change_b = halo(SECOND, second, near, edge, fixed_a, fixed_b)
    got_a, got_b = across(change_a, change_b)
    before, weighted = call(mix_kernel, [VMEM] * 7, [planes, planes], [])(
        taken, from_a, from_b, mix_a, mix_b, wet, state
    )
    sums = (tracers * COARSE * TILES + 4, LANES)
    out, part = call(
        close_kernel,
        [HBM] + [VMEM] * 6,
        [adjoint.shape, (number, 8, LANES)],
        [planes, planes, sums, sums, adjoint.shape, edges]
        + [pltpu.SMEM(owners.shape, I32), pltpu.SemaphoreType.DMA((tracers + 1,))],
        [HBM, VMEM],
    )(pltpu.with_memory_space_constraint(owners, pltpu.HBM), change_a, change_b, got_a, got_b, before, weighted)
    part = lax.all_to_all(part, "tiles", 0, 0, tiled=True)
    gradient = part.sum(axis=0).reshape(1, 1, 8 * LANES)[:, :, : tracers * COARSE * COARSE]
    return out, gradient


def solution(mesh):
    placed = (
        P("slab", None, "tiles", None),
        P("slab", None, "tiles", None),
        P("slab", "tiles", None),
        P("slab", "tiles", None),
        P("slab", "tiles", None),
        P(None, "tiles", None),
        P("tiles", None),
        P("tiles", None),
        P(),
    )
    return jax.shard_map(
        shards,
        mesh=mesh,
        in_specs=placed,
        out_specs=(P("slab", None, "tiles", None), P("slab", "tiles", None)),
        check_vma=False,
    )
```

```python
import jax
import jax.numpy as jnp
from jax import lax
from jax.experimental import pallas as pl
from jax.experimental.pallas import tpu as pltpu
from jax.sharding import PartitionSpec as P

TILE = 90
CELLS = TILE * TILE
BLOCK = 6
COARSE = 15
LANES = 128
COLS = 32
HALF = COLS * LANES
TILES = 4
SIDES = 4
SPOTS = TILES * SIDES
CHANNELS = 4
ROWS = SPOTS * CHANNELS
TILE_ROWS = SIDES * CHANNELS
SHOWN = ROWS + TILE_ROWS
ODD = 0
EVEN = SHOWN
OWN = 2 * SHOWN
OTHER = 3 * SHOWN
CLOSED = -8
TURNED = 1 << 16
FIRST_HIGH = HALF // TILE
UNROLL = 32
F32 = jnp.float32
I32 = jnp.int32


def position():
    lane = lax.broadcasted_iota(I32, (8, LANES), 1)
    low = lax.broadcasted_iota(I32, (8, LANES), 0) < TILES
    return lane, low


def cell_at(lane, low, v):
    cell = lane + jnp.where(low, 0, HALF) + v * LANES
    y = (cell * 46604) >> 22
    return cell - y * TILE, y


def lane_gather(values, index):
    return jnp.take_along_axis(values, index, axis=1, mode="promise_in_bounds")


def loop(body, carry=0):
    return lax.fori_loop(0, COLS, body, carry, unroll=UNROLL)


def fold(read, write):
    for v in range(COLS):
        write(v, 0, read(v * LANES, LANES))
        start = HALF + v * LANES
        width = min(LANES, CELLS - start)
        part = read(start, width)
        if width < LANES:
            part = jnp.concatenate([part, jnp.zeros((TILES, LANES - width), F32)], axis=1)
        write(v, TILES, part)


def set_guards(ref, plane, low):
    first, last = ref[plane, 1], ref[plane, COLS]
    ref[plane, 0] = jnp.where(low, 0.0, pltpu.roll(last, TILES, 0))
    ref[plane, COLS + 1] = jnp.where(low, pltpu.roll(first, TILES, 0), 0.0)


def inner_sum(ref, plane, v, lane, west, east):
    before, here, after = ref[plane, v], ref[plane, v + 1], ref[plane, v + 2]
    left = pltpu.roll(jnp.where(lane < LANES - 1, here, before), 1, 1)
    right = pltpu.roll(jnp.where(lane >= 1, here, after), LANES - 1, 1)
    up = pltpu.roll(jnp.where(lane < LANES - TILE, here, before), TILE, 1)
    down = pltpu.roll(jnp.where(lane >= TILE, here, after), LANES - TILE, 1)
    return jnp.where(west, 0.0, left) + jnp.where(east, 0.0, right) + (up + down)


def edge_sides(load, planes, lane, low):
    step = lane & 63
    base = TILE * step + jnp.where(low, 0, FIRST_HIGH * TILE - HALF) + jnp.where(lane < 64, TILE - 1, TILE)
    index, column = base & (LANES - 1), base >> 7

    def body(v, found):
        hit = column == v
        return tuple(jnp.where(hit, lane_gather(load(p, v), index), found[p]) for p in range(planes))

    found = loop(body, tuple(jnp.zeros((8, LANES), F32) for _ in range(planes)))
    bottom = CELLS - TILE - HALF + lane
    edge = lane < TILE
    first_low = jnp.where(low, lane + 63, lane - FIRST_HIGH + 63) & (LANES - 1)
    last_low = jnp.where(low, lane, lane - FIRST_HIGH) & (LANES - 1)
    out = []
    for p in range(planes):
        top = load(p, 0)
        picked = jnp.where(
            (bottom >> 7) == COLS - 2,
            lane_gather(load(p, COLS - 2), bottom & (LANES - 1)),
            lane_gather(load(p, COLS - 1), bottom & (LANES - 1)),
        )
        west, east = lane_gather(found[p], first_low), lane_gather(found[p], last_low)
        west = jnp.where(low, jnp.where(lane == 0, top, west), west)
        west_low, east_low = west[:TILES], east[:TILES]
        here = lane[:TILES]
        west = jnp.where(here <= FIRST_HIGH, west_low, west[TILES:])
        east = jnp.where(here < FIRST_HIGH, east_low, east[TILES:])
        inside = here < TILE
        out.append(
            [
                jnp.where(inside, top[:TILES], 0.0),
                jnp.where(inside, picked[TILES:], 0.0),
                jnp.where(inside, west, 0.0),
                jnp.where(inside, east, 0.0),
            ]
        )
    return out


def put_sides(ref, channel, sides):
    for s in range(SIDES):
        ref[pl.ds(s * CHANNELS + channel, TILES, stride=SIDES * CHANNELS), :] = sides[s]


def put_given(edge_ref, give_ref):
    first, last = edge_ref[pl.ds(0, TILE_ROWS), :], edge_ref[pl.ds(ROWS - TILE_ROWS, TILE_ROWS), :]
    start = lax.axis_index("tiles") % 2 == 0
    give_ref[pl.ds(0, TILE_ROWS), :] = jnp.where(start, first, last)
    give_ref[pl.ds(TILE_ROWS, TILE_ROWS), :] = jnp.where(start, last, first)


def channel_rows(ref, channel):
    return ref[pl.ds(channel, SPOTS, stride=CHANNELS), :]


def halo_places(table_ref, out_ref):
    me = lax.axis_index("tiles")
    chip, core = me // 2, me % 2
    even = chip % 2 == 0
    places = []
    for t in range(TILES):
        for s in range(SIDES):
            code = table_ref[t, s]
            tile, link = code >> 3, code & 7
            device, inner = tile // TILES, tile % TILES
            step = device // 2 - chip
            start = jnp.where((step == 1) == even, EVEN, ODD)
            own = jnp.where(device == me, OWN + inner * TILE_ROWS, OTHER)
            beside = start + jnp.where(device % 2 == core, inner * TILE_ROWS, ROWS)
            row = jnp.where(step == 0, own, beside) + (link // 2) * CHANNELS
            places.append(jnp.where(code < 0, CLOSED, row + (link % 2) * TURNED))
    _, low = position()
    channel = lax.broadcasted_iota(I32, (8, LANES), 0) % CHANNELS
    for k in range(0, SPOTS, 2):
        out_ref[pl.ds(k * CHANNELS, 8), :] = jnp.where(low, places[k], places[k + 1]) + channel


def halos(place_ref, all_ref, out_ref):
    lane, _ = position()
    back = jnp.clip(TILE - 1 - lane, 0, LANES - 1)
    for t in range(TILES):
        starts = [start + t * TILE_ROWS for start in (ODD, EVEN)]
        starts += [OWN + k * TILE_ROWS for k in (t - 1, t + 1) if 0 <= k < TILES]
        if t in (0, TILES - 1):
            starts += [OTHER, ODD + ROWS, EVEN + ROWS]
        chunks = [start // 8 + k for start in starts for k in range(TILE_ROWS // 8)]
        for h in range(TILE_ROWS // 8):
            at = pl.ds(t * TILE_ROWS + h * 8, 8)
            place = place_ref[at, :]
            chunk, row = (place & (TURNED - 1)) >> 3, place & 7
            found = jnp.zeros((8, LANES), F32)
            for k in chunks:
                picked = jnp.take_along_axis(all_ref[pl.ds(k * 8, 8), :], row, axis=0, mode="promise_in_bounds")
                found = jnp.where(chunk == k, picked, found)
            found = jnp.where((place >> 16) == 1, lane_gather(found, back), found)
            out_ref[at, :] = jnp.where(lane < TILE, found, 0.0)


def change_planes(own_a, own_b, got_a, got_b, tracers, scratch, lane, low):
    mix_a = channel_rows(own_a, tracers) * channel_rows(got_a, tracers)
    mix_b = channel_rows(own_b, tracers) * channel_rows(got_b, tracers)
    for c in range(tracers):
        own = channel_rows(own_a, c)
        scratch[pl.ds(c * SPOTS, SPOTS), :] = (
            own + mix_a * (channel_rows(got_a, c) - own) + mix_b * (channel_rows(got_b, c) - own)
        )
    out = []
    for c in range(tracers):
        sides = [scratch[pl.ds(c * SPOTS + s, TILES, stride=SIDES), :] for s in range(SIDES)]
        sides = [jnp.concatenate([side, side], axis=0) for side in sides]
        west = jnp.where(low, pltpu.roll(sides[2], 63, 1), pltpu.roll(sides[2], 63 - FIRST_HIGH, 1))
        east = jnp.where(low, sides[3], pltpu.roll(sides[3], LANES - FIRST_HIGH, 1))
        out.append([sides[0], sides[1], jnp.where(lane < 63, east, west)])
    return out


def add_columns(planes, v, lane, low):
    x, y = cell_at(lane, low, v)
    west, east = x == 0, x == TILE - 1
    index = (y + jnp.where(west, 63, 0) - jnp.where(low, 0, FIRST_HIGH)) & (LANES - 1)
    edge = west | east
    return [jnp.where(edge, lane_gather(sides[2], index), 0.0) for sides in planes]


def add_rows(ref, planes, lane, low):
    place = (CELLS - TILE - HALF) % LANES
    for c, sides in enumerate(planes):
        ref[c, 0] = ref[c, 0] + jnp.where(low, sides[0], 0.0)
        turned = pltpu.roll(sides[1], place, 1)
        ref[c, COLS - 2] = ref[c, COLS - 2] + jnp.where(low | (lane < place), 0.0, turned)
        ref[c, COLS - 1] = ref[c, COLS - 1] + jnp.where(low | (lane >= place + TILE - LANES), 0.0, turned)


def write_to(ref, *lead):
    def write(v, row, part):
        ref[(*lead, v, pl.ds(row, TILES), slice(None))] = part

    return write


def open_kernel(
    adjoint_hbm, weights_hbm, mask_hbm, near_hbm, link_hbm,
    edge_ref, give_ref, lam_ref, wet_ref, mixing_ref, spread, table_ref,
    adjoint_ref, weights_ref, mask_ref, near_ref, link_ref, sems,
):
    tracers = lam_ref.shape[0]
    pairs = (
        (mask_hbm, mask_ref),
        (weights_hbm, weights_ref),
        (adjoint_hbm, adjoint_ref),
        (near_hbm, near_ref),
        (link_hbm, link_ref),
    )
    copies = [pltpu.make_async_copy(source, target, sems.at[i]) for i, (source, target) in enumerate(pairs)]
    for copy in copies:
        copy.start()
    lane, low = position()
    copies[0].wait()
    fold(lambda a, n: mask_ref[0, :, a : a + n].astype(F32), write_to(wet_ref))
    copies[1].wait()
    fold(lambda a, n: weights_ref[0, :, a : a + n], write_to(mixing_ref))
    copies[2].wait()
    for c in range(tracers):
        fold(lambda a, n, c=c: adjoint_ref[0, c, :, a : a + n], write_to(lam_ref, c))

    def start(v, carry):
        wet = wet_ref[v]
        mixing = wet * mixing_ref[v]
        mixing_ref[v] = mixing
        for c in range(tracers):
            spread[c, v + 1] = mixing * lam_ref[c, v]
        spread[tracers, v + 1] = wet
        return carry

    loop(start)
    for c in range(tracers + 1):
        set_guards(spread, c, low)
    for p, sides in enumerate(edge_sides(lambda p, v: spread[p, v + 1], tracers + 1, lane, low)):
        put_sides(edge_ref, p, sides)
    put_given(edge_ref, give_ref)
    copies[3].wait()
    copies[4].wait()
    table_ref[...] = near_ref[...] * 8 + link_ref[...]


def inner_first_kernel(spread, lam_ref, wet_ref, mixing_ref, vertical_ref, rate_ref, pack_a, pack_b, stay_ref, keep_ref):
    tracers = lam_ref.shape[0]
    level, levels = lax.axis_index("slab"), lax.axis_size("slab")
    even = level % 2 == 0
    has_a = (level // 2 * 2 + 1 < levels).astype(F32)
    has_b = ((level >= 1) & ((level + 1) // 2 * 2 < levels)).astype(F32)
    for_a = has_a * jnp.where(even, 1.0, 0.0), has_a * jnp.where(even, 0.0, 1.0)
    for_b = has_b * jnp.where(even, 0.0, 1.0), has_b * jnp.where(even, 1.0, 0.0)
    lane, low = position()
    fold(lambda a, n: vertical_ref[0, :, a : a + n], write_to(stay_ref))
    for c in range(tracers):
        fold(lambda a, n, c=c: 1.0 - rate_ref[c, :, a : a + n], write_to(keep_ref, c))

    def body(v, carry):
        x, _ = cell_at(lane, low, v)
        west, east = x == 0, x == TILE - 1
        wet, vertical = wet_ref[v], stay_ref[v]
        pack_a[tracers, v] = wet * (for_a[0] + for_a[1] * vertical)
        pack_b[tracers, v] = wet * (for_b[0] + for_b[1] * vertical)
        stay = 1.0 - mixing_ref[v] * inner_sum(spread, tracers, v, lane, west, east)
        stay_ref[v] = stay
        for c in range(tracers):
            moved = inner_sum(spread, c, v, lane, west, east)
            taken = (lam_ref[c, v] * stay + wet * moved) * keep_ref[c, v]
            pack_a[c, v] = taken
            pack_b[c, v] = taken
        return carry

    loop(body)


def inner_kernel(spread, lam_ref, wet_ref, stay_ref, keep_ref, out_ref):
    tracers = lam_ref.shape[0]
    lane, low = position()

    def body(v, carry):
        x, _ = cell_at(lane, low, v)
        west, east = x == 0, x == TILE - 1
        wet, stay = wet_ref[v], stay_ref[v]
        for c in range(tracers):
            moved = inner_sum(spread, c, v, lane, west, east)
            out_ref[c, v] = (lam_ref[c, v] * stay + wet * moved) * keep_ref[c, v]
        return carry

    loop(body)


def fixed_kernel(table_ref, keep_ref, pack_a, pack_b, out_a, out_b, place_ref):
    tracers = keep_ref.shape[0]
    lane, low = position()
    halo_places(table_ref, place_ref)

    def load(p, v):
        return keep_ref[p, v] if p < tracers else (pack_a if p == tracers else pack_b)[tracers, v]

    found = edge_sides(load, tracers + 2, lane, low)
    for c in range(tracers):
        put_sides(out_a, c, found[c])
        put_sides(out_b, c, found[c])
    put_sides(out_a, tracers, found[tracers])
    put_sides(out_b, tracers, found[tracers + 1])


def halo_kernel(place_ref, all_ref, edge_ref, fixed_a, fixed_b, out_a, out_b, halo_ref):
    tracers = CHANNELS - 1
    halos(place_ref, all_ref, halo_ref)
    wet, halo_wet = channel_rows(edge_ref, tracers), channel_rows(halo_ref, tracers)
    for c in range(tracers):
        change = channel_rows(fixed_a, c) * (wet * channel_rows(halo_ref, c) - channel_rows(edge_ref, c) * halo_wet)
        for out in (out_a, out_b):
            out[pl.ds(c, SPOTS, stride=CHANNELS), :] = change
    out_a[pl.ds(tracers, SPOTS, stride=CHANNELS), :] = channel_rows(fixed_a, tracers)
    out_b[pl.ds(tracers, SPOTS, stride=CHANNELS), :] = channel_rows(fixed_b, tracers)


def mix_first_kernel(pack_a, pack_b, from_b, from_a, lam_ref, mix_a_ref, mix_b_ref):
    tracers = lam_ref.shape[0]

    def body(v, carry):
        first, second = pack_a[tracers, v] * from_a[tracers, v], pack_b[tracers, v] * from_b[tracers, v]
        mix_a_ref[v] = first
        mix_b_ref[v] = second
        for c in range(tracers):
            taken = pack_a[c, v]
            lam_ref[c, v] = taken + first * (from_a[c, v] - taken) + second * (from_b[c, v] - taken)
        return carry

    loop(body)


def mix_kernel(taken_ref, from_a, from_b, mix_a_ref, mix_b_ref, wet_ref, state_ref, lam_ref, term_ref):
    tracers = lam_ref.shape[0]
    for c in range(tracers):
        fold(lambda a, n, c=c: state_ref[0, c, :, a : a + n], write_to(term_ref, c))

    def body(v, carry):
        first, second, wet = mix_a_ref[v], mix_b_ref[v], wet_ref[v]
        for c in range(tracers):
            taken = taken_ref[c, v]
            lam_ref[c, v] = taken + first * (from_a[c, v] - taken) + second * (from_b[c, v] - taken)
            term_ref[c, v] = wet * term_ref[c, v]
        return carry

    loop(body)


def middle_kernel(
    change_a, change_b, got_a, got_b, before_ref, mixing_ref, wet_edge_ref, edge_ref, give_ref, lam_ref, spread, scratch
):
    tracers = lam_ref.shape[0]
    lane, low = position()
    planes = change_planes(change_a, change_b, got_a, got_b, tracers, scratch, lane, low)

    def body(v, carry):
        extra = add_columns(planes, v, lane, low)
        mixing = mixing_ref[v]
        for c in range(tracers):
            lam = before_ref[c, v] + extra[c]
            lam_ref[c, v] = lam
            spread[c, v + 1] = mixing * lam
        return carry

    loop(body)
    add_rows(lam_ref, planes, lane, low)
    for c in range(tracers):
        for v in (0, COLS - 2, COLS - 1):
            spread[c, v + 1] = mixing_ref[v] * lam_ref[c, v]
        set_guards(spread, c, low)
    for p, sides in enumerate(edge_sides(lambda p, v: spread[p, v + 1], tracers, lane, low)):
        put_sides(edge_ref, p, sides)
    edge_ref[pl.ds(tracers, SPOTS, stride=CHANNELS), :] = channel_rows(wet_edge_ref, tracers)
    put_given(edge_ref, give_ref)


def close_kernel(
    owner_hbm, change_a, change_b, got_a, got_b, before_ref, weighted_ref,
    out_hbm, part_ref, lam_ref, term_ref, rows_ref, sums_ref, flat_ref, scratch, owner_ref, sems,
):
    tracers = lam_ref.shape[0]
    owner_copy = pltpu.make_async_copy(owner_hbm, owner_ref, sems.at[tracers])
    owner_copy.start()
    lane, low = position()
    planes = change_planes(change_a, change_b, got_a, got_b, tracers, scratch, lane, low)

    def body(v, carry):
        extra = add_columns(planes, v, lane, low)
        for c in range(tracers):
            lam = before_ref[c, v] + extra[c]
            lam_ref[c, v] = lam
            term_ref[c, v] = weighted_ref[c, v] * lam
        return carry

    loop(body)
    add_rows(lam_ref, planes, lane, low)
    for c in range(tracers):
        for v in (0, COLS - 2, COLS - 1):
            term_ref[c, v] = weighted_ref[c, v] * lam_ref[c, v]
    copies = []
    for c in range(tracers):
        for v in range(COLS):
            values = lam_ref[c, v]
            flat_ref[0, c, :, v * LANES : (v + 1) * LANES] = values[:TILES]
            start = HALF + v * LANES
            width = min(LANES, CELLS - start)
            flat_ref[0, c, :, start : start + width] = values[TILES:, :width]
        copies.append(pltpu.make_async_copy(flat_ref.at[0, c], out_hbm.at[0, c], sems.at[c]))
        copies[-1].start()
    for c in range(tracers):
        guard = pltpu.roll(term_ref[c, 0], TILES, 0)
        for block in range(COARSE):
            total = [None, None]
            for y in range(block * BLOCK, (block + 1) * BLOCK):
                half = y * TILE // HALF
                v, shift = divmod(y * TILE - half * HALF, LANES)
                values = term_ref[c, v]
                if shift + TILE > LANES:
                    after = term_ref[c, v + 1] if v + 1 < COLS else guard
                    values = jnp.where(lane >= shift, values, after)
                if shift:
                    values = pltpu.roll(values, LANES - shift, 1)
                total[half] = values if total[half] is None else total[half] + values
            parts = [total[h][h * TILES : (h + 1) * TILES] for h in range(2) if total[h] is not None]
            summed = parts[0] if len(parts) == 1 else parts[0] + parts[1]
            summed = jnp.where(lane[:TILES] < TILE, summed, 0.0)
            rows_ref[pl.ds((c * COARSE + block) * TILES, TILES), :] = summed
    lane_in = lax.broadcasted_iota(I32, (LANES, LANES), 0)
    lane_out = lax.broadcasted_iota(I32, (LANES, LANES), 1)
    low_edge = lane_out * BLOCK
    pick = ((lane_in >= low_edge) & (lane_in < low_edge + BLOCK) & (lane_out < COARSE)).astype(jnp.bfloat16)
    left = rows_ref[...]
    summed = jnp.zeros_like(left)
    for _ in range(3):
        part = left.astype(jnp.bfloat16)
        summed = summed + jnp.dot(part, pick, preferred_element_type=F32)
        left = left - part.astype(F32)
    sums_ref[...] = summed
    for spot in range(8):
        total = jnp.zeros((TILES, LANES), F32)
        for k in range(tracers * COARSE):
            start = k * COARSE - spot * LANES
            if start >= LANES or start + COARSE <= 0:
                continue
            values = sums_ref[pl.ds(k * TILES, TILES), :]
            values = pltpu.roll(values, start % LANES, 1) if start % LANES else values
            if start < 0:
                values = jnp.where(lane[:TILES] < start + COARSE, values, 0.0)
            elif start + COARSE > LANES:
                values = jnp.where(lane[:TILES] >= start, values, 0.0)
            total = total + values
        rows_ref[pl.ds(spot, TILES, stride=8), :] = total
    part_ref[...] = jnp.zeros_like(part_ref)
    me = lax.axis_index("tiles")
    owner_copy.wait()
    for t in range(TILES):
        owner = owner_ref[me * TILES + t]
        part_ref[owner] = part_ref[owner] + rows_ref[pl.ds(t * 8, 8), :]
    for copy in copies:
        copy.wait()


def swaps(count, width=1):
    found = []
    for first in (0, 1):
        found.append(
            [
                pair
                for i in range(first, count // width - 1, 2)
                for k in range(width)
                for pair in ((i * width + k, (i + 1) * width + k), ((i + 1) * width + k, i * width + k))
            ]
        )
    return found


VMEM, SMEM, HBM = (pl.BlockSpec(memory_space=space) for space in (pltpu.VMEM, pltpu.SMEM, pltpu.HBM))


def call(kernel, ins, out, scratch, outs=None):
    return pl.pallas_call(
        kernel,
        out_shape=[jax.ShapeDtypeStruct(shape, F32) if isinstance(shape, tuple) else shape for shape in out],
        in_specs=ins,
        out_specs=outs or [VMEM] * len(out),
        scratch_shapes=[pltpu.VMEM(shape, F32) if isinstance(shape, tuple) else shape for shape in scratch],
        compiler_params=pltpu.CompilerParams(vmem_limit_bytes=32 * 1024 * 1024),
        name=kernel.__name__,
    )


def shards(adjoint, state, weights, vertical, mask, rate, neighbours, links, owners):
    tracers = adjoint.shape[1]
    number = lax.axis_size("tiles")
    levels = lax.axis_size("slab")
    even_swap, odd_swap = ([(k * levels + i, k * levels + j) for i, j in pairs for k in range(number)] for pairs in swaps(levels))
    core_swap = [(2 * i + a, 2 * i + 1 - a) for i in range(number // 2) for a in range(2)]
    for pairs in (even_swap, odd_swap):
        alone = set(range(levels)) - {i % levels for i, _ in pairs}
        pairs.extend((a * levels + i, b * levels + i) for i in sorted(alone) for a, b in core_swap)
    even_chips, odd_chips = swaps(number, 2)
    odd_chips += [pair for k in range(2) for pair in ((k, number - 2 + k), (number - 2 + k, k))]
    plane = (COLS, 8, LANES)
    planes = (tracers, *plane)
    pack = (tracers + 1, *plane)
    guarded = (COLS + 2, 8, LANES)
    edges = (ROWS, LANES)
    given = (2 * TILE_ROWS, LANES)

    def around(edge, other):
        shown = jnp.concatenate([edge, other[:TILE_ROWS]])
        even = lax.ppermute(shown, "tiles", even_chips)
        odd = lax.ppermute(shown, "tiles", odd_chips)
        return jnp.concatenate([odd, even, shown, other[TILE_ROWS:]])

    def across(first, second):
        return lax.ppermute(first, ("tiles", "slab"), even_swap), lax.ppermute(second, ("tiles", "slab"), odd_swap)

    edge, give, lam, wet, mixing, spread, table = call(
        open_kernel,
        [HBM] * 5,
        [edges, given, planes, plane, plane, (tracers + 1, *guarded), jax.ShapeDtypeStruct(links.shape, I32)],
        [adjoint.shape, weights.shape]
        + [pltpu.VMEM(table.shape, I32) for table in (mask, neighbours, links)]
        + [pltpu.SemaphoreType.DMA((5,))],
    )(*(pltpu.with_memory_space_constraint(x, pltpu.HBM) for x in (adjoint, weights, mask, neighbours, links)))
    other = lax.ppermute(give, "tiles", core_swap)
    pack_a, pack_b, stay, keep = call(inner_first_kernel, [VMEM] * 6, [pack, pack, plane, planes], [])(
        spread, lam, wet, mixing, vertical, rate
    )
    from_a, from_b = across(pack_a, pack_b)
    near = around(edge, other)
    fixed_a, fixed_b, places = call(
        fixed_kernel, [SMEM] + [VMEM] * 3, [edges] * 2 + [jax.ShapeDtypeStruct(edges, I32)], []
    )(table, keep, pack_a, pack_b)

    halo = call(halo_kernel, [VMEM] * 5, [edges] * 2, [edges])
    change_a, change_b = halo(places, near, edge, fixed_a, fixed_b)
    got_a, got_b = across(change_a, change_b)
    before, mix_a, mix_b = call(mix_first_kernel, [VMEM] * 4, [planes, plane, plane], [])(
        pack_a, pack_b, from_b, from_a
    )
    edge, give, lam, spread = call(middle_kernel, [VMEM] * 7, [edges, given, planes, (tracers, *guarded)], [edges])(
        change_a, change_b, got_a, got_b, before, mixing, edge
    )
    other = lax.ppermute(give, "tiles", core_swap)
    (taken,) = call(inner_kernel, [VMEM] * 5, [planes], [])(spread, lam, wet, stay, keep)
    taken, other = lax.optimization_barrier((taken, other))
    from_a, from_b = across(taken, taken)
    near = around(edge, other)
    change_a, change_b = halo(places, near, edge, fixed_a, fixed_b)
    got_a, got_b = across(change_a, change_b)
    before, weighted = call(mix_kernel, [VMEM] * 7, [planes, planes], [])(
        taken, from_a, from_b, mix_a, mix_b, wet, state
    )
    sums = (tracers * COARSE * TILES + 4, LANES)
    out, part = call(
        close_kernel,
        [HBM] + [VMEM] * 6,
        [adjoint.shape, (number, 8, LANES)],
        [planes, planes, sums, sums, adjoint.shape, edges]
        + [pltpu.SMEM(owners.shape, I32), pltpu.SemaphoreType.DMA((tracers + 1,))],
        [HBM, VMEM],
    )(pltpu.with_memory_space_constraint(owners, pltpu.HBM), change_a, change_b, got_a, got_b, before, weighted)
    part = lax.all_to_all(part, "tiles", 0, 0, tiled=True)
    gradient = part.sum(axis=0).reshape(1, 1, 8 * LANES)[:, :, : tracers * COARSE * COARSE]
    return out, gradient


def solution(mesh):
    placed = (
        P("slab", None, "tiles", None),
        P("slab", None, "tiles", None),
        P("slab", "tiles", None),
        P("slab", "tiles", None),
        P("slab", "tiles", None),
        P(None, "tiles", None),
        P("tiles", None),
        P("tiles", None),
        P(),
    )
    return jax.shard_map(
        shards,
        mesh=mesh,
        in_specs=placed,
        out_specs=(P("slab", None, "tiles", None), P("slab", "tiles", None)),
        check_vma=False,
    )
```
